512 devices in a mesh: dp: 128 (over z, y, core), tm: 4 (over x).
Axes of the slice: x: 4, y: 8, z: 8, core: 2. Of those that a mesh axis runs over, the one named last changes fastest.
Arguments:
- lengths: int32 [128], P('dp'), may hold values from 17 to 33
- frames: bfloat16 [128, 36, 256, 256], P('dp', 'tm'), may hold values from -6 to 6
- weights: bfloat16 [3, 256, 256], replicated, may hold values from -0.21875 to 0.21875
- cotangent: bfloat16 [128, 36, 256, 256], P('dp', 'tm'), may hold values from -6 to 6
Outputs:
- output: bfloat16 [128, 36, 256, 256], P('dp', 'tm')
- input_grad: bfloat16 [128, 36, 256, 256], P('dp', 'tm')
- weight_grad: float32 [3, 256, 256], replicated
The draws below stay inside these ranges and needn't reach their ends.
Inputs may be any that keep to these rules, and one draw needn't show every extreme that they name: `lengths`: each clip length lies between half the frame slots less one and the frame slots less three.
All inputs are finite; a program needn't handle non-finite values.
Results may differ from the reference program's by a relative error of at most 0.0049.
Values may be sent and summed in bfloat16 or wider, within the bound.
No kernel may reach another device: no remote copies, remote signals or barrier semaphores. Data moves between devices by JAX's collectives and lax.ppermute only.
A program may use at most 64 MiB of HBM per device.

```python
import jax
import jax.numpy as jnp
from jax import lax

C = 256
PIX = 256
F_CAP = 36
CLIPS = 128


def with_ends(values, key, smallest, top_value):
    shape = values.shape
    spot = [jax.random.randint(jax.random.fold_in(key, axis), (), 0, shape[axis]) for axis in range(len(shape))]
    values = values.at[tuple(spot)].set(smallest)
    longest = shape.index(max(shape))
    spot[longest] = (spot[longest] + 1) % shape[longest]
    return values.at[tuple(spot)].set(top_value)


def levels(own_key, dims, shards, smallest, top_value):
    level, own = 1.0, jax.random.fold_in(own_key, 6)
    for position, parts in shards:
        heights = jnp.exp(jax.random.uniform(jax.random.fold_in(own, position), (parts,), jnp.float32, smallest / len(shards), top_value / len(shards)))
        level = level * jnp.repeat(heights, dims[position] // parts).reshape([-1 if axis == position else 1 for axis in range(len(dims))])
    return level


def bell_draw(rng, dims, deviation, limit, pieces=(), held_as=jnp.bfloat16):
    loudness = levels(rng, dims, pieces, -0.22, 0.18) if pieces else 1.0
    values = jax.random.normal(rng, dims, jnp.float32) * deviation * loudness
    return jnp.minimum(jnp.maximum(values, -limit), limit).astype(held_as)


def setup_inputs(seed: int = 0) -> dict:
    keys = jax.random.split(jax.random.key(seed), 5)
    return {
        "lengths": with_ends(jax.random.randint(keys[0], (CLIPS,), F_CAP // 2 - 1, F_CAP - 2), jax.random.fold_in(keys[0], 1), F_CAP // 2 - 1, (F_CAP - 2) - 1).astype(jnp.int32),
        "frames": bell_draw(keys[1], (CLIPS, F_CAP, PIX, C), 1.0, 6.0, ((0, 128), (1, 4))),
        "weights": bell_draw(keys[2], (3, C, C), (3 * C) ** -0.5, 0.21875),
        "cotangent": bell_draw(keys[3], (CLIPS, F_CAP, PIX, C), 1.0, 6.0, ((0, 128), (1, 4))),
    }


def one_clip(length, clip, cot, weights):
    valid = (jnp.arange(F_CAP) < length).astype(jnp.bfloat16)[:, None, None]
    masked = clip * valid
    padded = jnp.concatenate([jnp.zeros((2, PIX, C), jnp.bfloat16), masked], 0)
    pre = jnp.zeros((F_CAP * PIX, C), jnp.float32)
    for tap in range(3):
        shifted = padded[2 - tap:2 - tap + F_CAP].reshape(F_CAP * PIX, C)
        pre = pre + jnp.dot(shifted, weights[tap], preferred_element_type=jnp.float32)
    pre = pre.reshape(F_CAP, PIX, C)
    vf = valid.astype(jnp.float32)
    sig = jax.nn.sigmoid(pre)
    output = (vf * pre * sig).astype(jnp.bfloat16)
    grad_pre = (vf * cot.astype(jnp.float32) * sig * (1.0 + pre * (1.0 - sig))).astype(jnp.bfloat16)
    flat_grad = grad_pre.reshape(F_CAP * PIX, C)
    wgrad = []
    for tap in range(3):
        shifted = padded[2 - tap:2 - tap + F_CAP].reshape(F_CAP * PIX, C)
        wgrad.append(lax.dot_general(shifted, flat_grad, (((0,), (0,)), ((), ())), preferred_element_type=jnp.float32))
    later = jnp.concatenate([grad_pre, jnp.zeros((2, PIX, C), jnp.bfloat16)], 0)
    back = jnp.zeros((F_CAP * PIX, C), jnp.float32)
    for tap in range(3):
        ahead = later[tap:tap + F_CAP].reshape(F_CAP * PIX, C)
        back = back + lax.dot_general(ahead, weights[tap], (((1,), (1,)), ((), ())), preferred_element_type=jnp.float32)
    input_grad = (vf * back.reshape(F_CAP, PIX, C)).astype(jnp.bfloat16)
    return (output, input_grad, jnp.stack(wgrad))

def reference(lengths, frames, weights, cotangent):

    def step(total, item):
        length, clip, cot = item
        output, input_grad, wgrad = one_clip(length, clip, cot, weights)
        return (total + wgrad, (output, input_grad))
    total, (output, input_grad) = lax.scan(step, jnp.zeros((3, C, C), jnp.float32), (lengths, frames, cotangent))
    scale = 1.0 / jnp.sqrt(jnp.float32(CLIPS * F_CAP * PIX))
    return (output, input_grad, total * scale)
```

```python
import functools
import math

import jax
import jax.numpy as jnp
from jax import lax
from jax.experimental import pallas as pl
from jax.experimental.pallas import tpu as pltpu
from jax.sharding import Mesh, PartitionSpec as P

VMEM_LIMIT = 40 * 1024 * 1024
VMEM = pl.BlockSpec(memory_space=pltpu.VMEM)
SMEM = pl.BlockSpec(memory_space=pltpu.SMEM)
HBM = pl.BlockSpec(memory_space=pl.ANY)
ROWS = (((1,), (0,)), ((), ()))
COLS = (((1,), (1,)), ((), ()))


def dot(a, b, dims=ROWS):
    return lax.dot_general(a, b, dims, preferred_element_type=jnp.float32)


def activate(pre, cot, keep):
    sig = 0.5 * jnp.tanh(0.5 * pre) + 0.5
    value = keep * (pre * sig)
    slope = (keep * cot.astype(jnp.float32)) * (sig * (1.0 + pre * (1.0 - sig)))
    return value.astype(jnp.bfloat16), slope.astype(jnp.bfloat16)


def body_kernel(
    left_ref, frames_hbm, cot_hbm, w_hbm, out_hbm, grad_hbm, wsum_ref,
    frames, cot, w, out, grad, flipped, in_sem, cot_sem, w_sem, out_sem, grad_sem,
):
    count = frames.shape[0]
    width = frames.shape[2]

    def frame_in(t):
        return pltpu.make_async_copy(frames_hbm.at[t], frames.at[t], in_sem.at[t])

    def cot_in(t):
        return pltpu.make_async_copy(cot_hbm.at[t], cot.at[t], cot_sem.at[t])

    def out_copy(t):
        return pltpu.make_async_copy(out.at[t], out_hbm.at[t], out_sem.at[t])

    def grad_copy(t):
        return pltpu.make_async_copy(grad.at[t], grad_hbm.at[t], grad_sem.at[t])

    w_in = pltpu.make_async_copy(w_hbm, w, w_sem)
    w_in.start()
    for t in range(3):
        frame_in(t).start()
    cot_in(2).start()
    for t in range(3, count):
        frame_in(t).start()
        cot_in(t).start()
    wsum_ref[...] = jnp.zeros_like(wsum_ref)
    w_in.wait()
    for t in range(2):
        frame_in(t).wait()
        flipped[t] = frames[t].T

    def step(t, carry):
        frame_in(t).wait()
        now = frames[t]
        pre = dot(now, w[0]) + dot(frames[t - 1], w[1]) + dot(frames[t - 2], w[2])
        flipped[t] = now.T
        cot_in(t).wait()
        keep = (t < left_ref[0]).astype(jnp.float32)
        value, slope = activate(pre, cot[t], keep)
        out[t] = value
        grad[t] = slope
        out_copy(t).start()
        grad_copy(t).start()
        for tap in range(3):
            part = pl.ds(tap * width, width)
            wsum_ref[part, :] += dot(flipped[t - tap], slope)
        return carry

    lax.fori_loop(2, count, step, 0)
    for t in range(2, count):
        out_copy(t).wait()
        grad_copy(t).wait()


def head_kernel(
    scale, left_ref, halo_ref, frames_ref, cot_ref, w_ref, wpart_ref, out_in, grad_in,
    out_ref, grad_ref, head_ref, terms_ref,
):
    del out_in, grad_in
    width = frames_ref.shape[2]
    group = terms_ref.shape[0]
    share = width // group
    back = [halo_ref[0], halo_ref[1], frames_ref[0], frames_ref[1]]
    flipped = [frame.T for frame in back]
    slopes = []
    for t in range(2):
        pre = dot(back[t + 2], w_ref[0]) + dot(back[t + 1], w_ref[1]) + dot(back[t], w_ref[2])
        keep = (t < left_ref[0]).astype(jnp.float32)
        value, slope = activate(pre, cot_ref[t], keep)
        out_ref[t] = value
        grad_ref[t] = slope
        head_ref[t] = slope
        slopes.append(slope)
    for tap in range(3):
        total = wpart_ref[tap * width : (tap + 1) * width, :]
        total = total + dot(flipped[2 - tap], slopes[0]) + dot(flipped[3 - tap], slopes[1])
        total = (total * scale).astype(jnp.bfloat16)
        for piece in range(group):
            terms_ref[piece, tap * share : (tap + 1) * share, :] = total[
                piece * share : (piece + 1) * share
            ]


def back_kernel(grad_hbm, halo_hbm, w_hbm, out_hbm, grad, w, out, in_sem, halo_sem, w_sem, out_sem):
    count = out.shape[0]

    def grad_in(t):
        return pltpu.make_async_copy(grad_hbm.at[t], grad.at[t], in_sem.at[t])

    def out_copy(t):
        return pltpu.make_async_copy(out.at[t], out_hbm.at[t], out_sem.at[t])

    halo_in = pltpu.make_async_copy(halo_hbm, grad.at[pl.ds(count, 2)], halo_sem)
    w_in = pltpu.make_async_copy(w_hbm, w, w_sem)
    w_in.start()
    for t in range(count):
        grad_in(t).start()
    halo_in.start()
    w_in.wait()
    grad_in(0).wait()
    grad_in(1).wait()

    def step(t, carry):
        @pl.when(t + 2 < count)
        def _():
            grad_in(t + 2).wait()

        @pl.when(t + 2 == count)
        def _():
            halo_in.wait()

        total = dot(grad[t], w[0], COLS) + dot(grad[t + 1], w[1], COLS) + dot(grad[t + 2], w[2], COLS)
        out[t] = total.astype(jnp.bfloat16)
        out_copy(t).start()
        return carry

    lax.fori_loop(0, count, step, 0)
    for t in range(count):
        out_copy(t).wait()


def first_sum_kernel(in_ref, out_ref):
    total = jnp.sum(in_ref[...].astype(jnp.float32), 0)
    pieces, rows, cols = out_ref.shape
    across = total.shape[1] // cols
    for piece in range(pieces):
        r, h = divmod(piece, across)
        out_ref[piece] = total[r * rows : (r + 1) * rows, h * cols : (h + 1) * cols].astype(
            jnp.bfloat16
        )


def spread_sum_kernel(in_ref, out_ref):
    total = jnp.sum(in_ref[...].astype(jnp.float32), 0).astype(jnp.bfloat16)
    for piece in range(out_ref.shape[0]):
        out_ref[piece] = total


def spread_kernel(in_ref, out_ref):
    pieces, rows, cols = in_ref.shape
    across = out_ref.shape[2] // cols
    total = in_ref[...].astype(jnp.float32)
    for r in range(pieces // across):
        line = jnp.concatenate([total[r * across + h] for h in range(across)], 1)
        for copy in range(out_ref.shape[0]):
            out_ref[copy, r * rows : (r + 1) * rows, :] = line.astype(jnp.bfloat16)


def last_kernel(in_ref, out_ref):
    group = in_ref.shape[0]
    share = out_ref.shape[1] // group
    for piece in range(group):
        for tap in range(3):
            out_ref[tap, piece * share : (piece + 1) * share, :] = in_ref[
                piece, tap * share : (tap + 1) * share, :
            ].astype(jnp.float32)


def call(kernel, out_shape, in_specs, out_specs, scratch=(), aliases={}, flops=0, moved=0):
    return pl.pallas_call(
        kernel,
        out_shape=out_shape,
        in_specs=in_specs,
        out_specs=out_specs,
        scratch_shapes=list(scratch),
        input_output_aliases=aliases,
        compiler_params=pltpu.CompilerParams(vmem_limit_bytes=VMEM_LIMIT),
        cost_estimate=pl.CostEstimate(flops=flops, bytes_accessed=moved, transcendentals=0),
    )


def small(kernel, value, shape, dtype=jnp.bfloat16):
    return call(kernel, jax.ShapeDtypeStruct(shape, dtype), [VMEM], VMEM, moved=2 * value.size)(value)


def passed_along(value, axis, steps):
    count = lax.axis_size(axis)
    first, last = (max(0, -steps), min(count, count - steps))
    return lax.ppermute(value, axis, [(source, source + steps) for source in range(first, last)])


def exchange(value, axes):
    return lax.all_to_all(value, axes, 0, 0, tiled=True)


def local(lengths, frames, weights, cotangent):
    bf16, f32 = jnp.bfloat16, jnp.float32
    clip, cot = frames[0], cotangent[0]
    count, pixels, chans = clip.shape
    left = lengths - lax.axis_index("x") * count
    frame = (count, pixels, chans)
    sds = jax.ShapeDtypeStruct
    dma = pltpu.SemaphoreType.DMA
    halo = passed_along(clip[count - 2 :], "x", 1)
    size = pixels * chans * 2
    work = 2 * pixels * chans * chans
    output, grad, wpart = call(
        body_kernel,
        (sds(frame, bf16), sds(frame, bf16), sds((3 * chans, chans), f32)),
        [SMEM, HBM, HBM, HBM],
        (HBM, HBM, VMEM),
        scratch=[
            pltpu.VMEM(frame, bf16),
            pltpu.VMEM(frame, bf16),
            pltpu.VMEM((3, chans, chans), bf16),
            pltpu.VMEM(frame, bf16),
            pltpu.VMEM(frame, bf16),
            pltpu.VMEM((count, chans, pixels), bf16),
            dma((count,)),
            dma((count,)),
            dma,
            dma((count,)),
            dma((count,)),
        ],
        flops=(count - 2) * 6 * work,
        moved=36 * size,
    )(left, clip, cot, weights)
    total_rows = lax.axis_size(("z", "y", "c", "x")) * count * pixels
    group = lax.axis_size(("c", "x"))
    two = pl.BlockSpec((2, pixels, chans), lambda i: (0, 0, 0))
    whole = lambda shape: pl.BlockSpec(shape, lambda i: (0,) * len(shape))
    terms_shape = (group, 3 * chans // group, chans)
    output, grad, head, terms = pl.pallas_call(
        functools.partial(head_kernel, 1.0 / math.sqrt(total_rows)),
        out_shape=(sds(frame, bf16), sds(frame, bf16), sds((2, pixels, chans), bf16), sds(terms_shape, bf16)),
        grid=(1,),
        in_specs=[
            SMEM, two, two, two, whole((3, chans, chans)), whole((3 * chans, chans)), HBM, HBM,
        ],
        out_specs=(two, two, two, whole(terms_shape)),
        input_output_aliases={6: 0, 7: 1},
        compiler_params=pltpu.CompilerParams(vmem_limit_bytes=VMEM_LIMIT),
        cost_estimate=pl.CostEstimate(flops=12 * work, bytes_accessed=16 * size, transcendentals=0),
    )(left, halo, clip, cot, weights, wpart, output, grad)

    following = passed_along(head, "x", -1)
    input_grad = call(
        back_kernel,
        sds(frame, bf16),
        [HBM, HBM, HBM],
        HBM,
        scratch=[
            pltpu.VMEM((count + 2, pixels, chans), bf16),
            pltpu.VMEM((3, chans, chans), bf16),
            pltpu.VMEM(frame, bf16),
            dma((count,)),
            dma,
            dma,
            dma((count,)),
        ],
        flops=count * 3 * work,
        moved=22 * size,
    )(grad, following, weights)

    ny, nz = lax.axis_size("y"), lax.axis_size("z")
    rows, cols = terms_shape[1] * chans // ny // 128, 128
    terms = exchange(terms, ("c", "x"))
    terms = small(first_sum_kernel, terms, (ny, rows, cols))
    terms = exchange(terms, "y")
    terms = small(spread_sum_kernel, terms, (nz, rows, cols))
    terms = exchange(terms, "z")
    terms = small(spread_sum_kernel, terms, (ny, rows, cols))
    terms = exchange(terms, "y")
    terms = small(spread_kernel, terms, terms_shape)
    terms = exchange(terms, ("c", "x"))
    weight_grad = small(last_kernel, terms, (3, chans, chans), f32)
    return (output[None], input_grad[None], weight_grad)


def solution(mesh):
    dp, tm = mesh.devices.shape
    side = math.isqrt(dp // 2)
    fine = Mesh(mesh.devices.reshape(side, -1, 2, tm), ("z", "y", "c", "x"))
    data = P(("z", "y", "c"), "x", None, None)
    in_specs = (P(("z", "y", "c")), data, P(), data)
    out_specs = (data, data, P())
    return jax.shard_map(local, mesh=fine, in_specs=in_specs, out_specs=out_specs, check_vma=False)
```

```python
import functools
import math

import jax
import jax.numpy as jnp
from jax import lax
from jax.experimental import pallas as pl
from jax.experimental.pallas import tpu as pltpu
from jax.sharding import Mesh, PartitionSpec as P

VMEM_LIMIT = 40 * 1024 * 1024
WIDE_LIMIT = 61 * 1024 * 1024
VMEM = pl.BlockSpec(memory_space=pltpu.VMEM)
SMEM = pl.BlockSpec(memory_space=pltpu.SMEM)
HBM = pl.BlockSpec(memory_space=pltpu.HBM)
ROWS = (((1,), (0,)), ((), ()))
COLS = (((1,), (1,)), ((), ()))


def dot(a, b, dims=ROWS):
    return lax.dot_general(a, b, dims, preferred_element_type=jnp.float32)


def activate(pre, cot, keep):
    sig = 0.5 * jnp.tanh(0.5 * pre) + 0.5
    value = keep * (pre * sig)
    slope = (keep * cot.astype(jnp.float32)) * (sig * (1.0 + pre * (1.0 - sig)))
    return value.astype(jnp.bfloat16), slope.astype(jnp.bfloat16)


def taps_of(frames, t, size):
    return jnp.concatenate([rows_of(frames[t - tap : t - tap + size]) for tap in range(3)], 1)


def rows_of(frames):
    return frames.reshape(-1, frames.shape[-1])


def body_kernel(
    left_ref, frames_hbm, cot_hbm, w_hbm, out_hbm, grad, wsum_ref,
    frames, cot, w, out, flipped, in_sem, cot_sem, w_sem, out_sem,
):
    count, pixels, width = frames.shape
    middle = 2 + (count - 2) // 2
    groups = [(2, middle), (middle, count)]
    copies = []
    for g, (start, end) in enumerate(groups):
        begin = 0 if g == 0 else start
        pair = []
        for source, target, sem, low in (
            (frames_hbm, frames, in_sem, begin), (cot_hbm, cot, cot_sem, start),
        ):
            part = pl.ds(low, end - low)
            pair.append(pltpu.make_async_copy(source.at[part], target.at[part], sem.at[g]))
        copies.append(pair)
    w_in = pltpu.make_async_copy(w_hbm, w, w_sem)
    copies[0][0].start()
    w_in.start()
    copies[0][1].start()
    copies[1][0].start()
    copies[1][1].start()
    copies[0][0].wait()
    w_in.wait()
    stacked = rows_of(w[...])
    pre = [dot(taps_of(frames, 2, middle - 2), stacked)]
    copies[0][1].wait()
    copies[1][0].wait()
    pre.append(dot(taps_of(frames, middle, count - middle), stacked))
    copies[1][1].wait()
    for t in range(count):
        flipped[:, t * pixels : (t + 1) * pixels] = frames[t].T
    total = None
    for g, (start, end) in enumerate(groups):
        slopes = []
        for t in range(start, end):
            rows = slice((t - start) * pixels, (t - start + 1) * pixels)
            keep = (t < left_ref[0]).astype(jnp.float32)
            value, slope = activate(pre[g][rows], cot[t], keep)
            out[t] = value
            grad[t] = slope
            slopes.append(slope)
        slope = jnp.concatenate(slopes, 0)
        for tap in range(3):
            term = dot(flipped[:, (start - tap) * pixels : (end - tap) * pixels], slope)
            part = slice(tap * width, (tap + 1) * width)
            wsum_ref[part, :] = term if g == 0 else wsum_ref[part, :] + term
    done = pltpu.make_async_copy(
        out.at[pl.ds(2, count - 2)], out_hbm.at[pl.ds(2, count - 2)], out_sem
    )
    done.start()
    done.wait()


def head_kernel(
    scale, left_ref, halo_hbm, frames_hbm, cot_hbm, w_hbm, wpart_hbm, out_in, out_hbm, head_ref, terms_ref,
    frames, cot, w, wpart, out, sems, out_sem,
):
    del out_in
    width = frames.shape[2]
    group = terms_ref.shape[0]
    share = width // group
    two = pl.ds(0, 2)
    copies = [
        pltpu.make_async_copy(source, target, sems.at[i])
        for i, (source, target) in enumerate(
            (
                (halo_hbm, frames.at[two]),
                (frames_hbm.at[two], frames.at[pl.ds(2, 2)]),
                (w_hbm, w),
                (cot_hbm.at[two], cot),
                (wpart_hbm, wpart),
            )
        )
    ]
    for copy in copies:
        copy.start()
    for copy in copies[:4]:
        copy.wait()
    pre = dot(taps_of(frames, 2, 2), rows_of(w[...]))
    flipped = [frames[t].T for t in range(4)]
    slopes = []
    for t in range(2):
        keep = (t < left_ref[0]).astype(jnp.float32)
        rows = slice(t * cot.shape[1], (t + 1) * cot.shape[1])
        value, slope = activate(pre[rows], cot[t], keep)
        out[t] = value
        head_ref[t] = slope
        slopes.append(slope)
    slope = jnp.concatenate(slopes, 0)
    out_copy = pltpu.make_async_copy(out, out_hbm.at[two], out_sem)
    out_copy.start()
    copies[4].wait()
    for tap in range(3):
        total = wpart[tap * width : (tap + 1) * width, :]
        total = total + dot(jnp.concatenate([flipped[2 - tap], flipped[3 - tap]], 1), slope)
        total = (total * scale).astype(jnp.bfloat16)
        for piece in range(group):
            terms_ref[piece, tap * share : (tap + 1) * share, :] = total[
                piece * share : (piece + 1) * share
            ]
    out_copy.wait()


def back_kernel(grad, head, halo, w, out_hbm, out, out_sem):
    count, pixels, width = out.shape
    weights = jnp.concatenate([w[tap].T for tap in range(3)], 0)
    size = 3
    for start in range(0, count, size):
        end = min(start + size, count)
        lines = []
        for tap in range(3):
            picked = []
            for t in range(start + tap, end + tap):
                picked.append(head[t] if t < 2 else grad[t] if t < count else halo[t - count])
            lines.append(jnp.concatenate(picked, 0))
        total = dot(jnp.concatenate(lines, 1), weights)
        out[start:end] = total.astype(jnp.bfloat16).reshape(end - start, pixels, width)
        part = pl.ds(start, end - start)
        pltpu.make_async_copy(out.at[part], out_hbm.at[part], out_sem.at[start // size]).start()
    for start in range(0, count, size):
        part = pl.ds(start, min(size, count - start))
        pltpu.make_async_copy(out.at[part], out_hbm.at[part], out_sem.at[start // size]).wait()


def sum_kernel(in_ref, *out_refs):
    total = jnp.sum(in_ref[...].astype(jnp.float32), 0)
    rows = out_refs[0].shape[0]
    for part, out_ref in enumerate(out_refs):
        out_ref[...] = total[part * rows : (part + 1) * rows]


def spread_kernel(*refs):
    *in_refs, out_ref = refs
    rows = in_refs[0].shape[0]
    for part, in_ref in enumerate(in_refs):
        value = in_ref[...].astype(jnp.bfloat16)
        for copy in range(out_ref.shape[0]):
            out_ref[copy, part * rows : (part + 1) * rows, :] = value


def last_kernel(in_ref, out_ref):
    group = in_ref.shape[0]
    share = out_ref.shape[1] // group
    for piece in range(group):
        for tap in range(3):
            out_ref[tap, piece * share : (piece + 1) * share, :] = in_ref[
                piece, tap * share : (tap + 1) * share, :
            ].astype(jnp.float32)


def call(kernel, out_shape, in_specs, out_specs, scratch=(), aliases={}, flops=0, moved=0, limit=VMEM_LIMIT):
    return pl.pallas_call(
        kernel,
        out_shape=out_shape,
        in_specs=in_specs,
        out_specs=out_specs,
        scratch_shapes=list(scratch),
        input_output_aliases=aliases,
        compiler_params=pltpu.CompilerParams(vmem_limit_bytes=limit),
        cost_estimate=pl.CostEstimate(flops=flops, bytes_accessed=moved, transcendentals=0),
    )


def small(kernel, value, shape, dtype=jnp.bfloat16):
    return call(kernel, jax.ShapeDtypeStruct(shape, dtype), [VMEM], VMEM, moved=2 * value.size)(value)


def passed_along(value, axis, steps):
    count = lax.axis_size(axis)
    first, last = (max(0, -steps), min(count, count - steps))
    return lax.ppermute(value, axis, [(source, source + steps) for source in range(first, last)])


def exchange(value, axes):
    return lax.all_to_all(value, axes, 0, 0, tiled=True)


def local(lengths, frames, weights, cotangent):
    bf16, f32 = jnp.bfloat16, jnp.float32
    clip, cot = frames[0], cotangent[0]
    count, pixels, chans = clip.shape
    left = lengths - lax.axis_index("x") * count
    frame = (count, pixels, chans)
    sds = jax.ShapeDtypeStruct
    dma = pltpu.SemaphoreType.DMA
    halo = passed_along(clip[count - 2 :], "x", 1)
    size = pixels * chans * 2
    work = 2 * pixels * chans * chans
    output, grad, wpart = call(
        body_kernel,
        (sds(frame, bf16), sds(frame, bf16), sds((3 * chans, chans), f32)),
        [SMEM, HBM, HBM, HBM],
        (HBM, VMEM, VMEM),
        scratch=[
            pltpu.VMEM(frame, bf16),
            pltpu.VMEM(frame, bf16),
            pltpu.VMEM((3, chans, chans), bf16),
            pltpu.VMEM(frame, bf16),
            pltpu.VMEM((chans, count * pixels), bf16),
            dma((2,)),
            dma((2,)),
            dma,
            dma,
        ],
        flops=(count - 2) * 6 * work,
        moved=36 * size,
        limit=WIDE_LIMIT,
    )(left, clip, cot, weights)
    total_rows = lax.axis_size(("z", "y", "c", "x")) * count * pixels
    group = lax.axis_size(("c", "x"))
    terms_shape = (group, 3 * chans // group, chans)
    output, head, terms = call(
        functools.partial(head_kernel, 1.0 / math.sqrt(total_rows)),
        (sds(frame, bf16), sds((2, pixels, chans), bf16), sds(terms_shape, bf16)),
        [SMEM, HBM, HBM, HBM, HBM, HBM, HBM],
        (HBM, VMEM, VMEM),
        scratch=[
            pltpu.VMEM((4, pixels, chans), bf16),
            pltpu.VMEM((2, pixels, chans), bf16),
            pltpu.VMEM((3, chans, chans), bf16),
            pltpu.VMEM((3 * chans, chans), f32),
            pltpu.VMEM((2, pixels, chans), bf16),
            dma((5,)),
            dma,
        ],
        aliases={6: 0},
        flops=12 * work,
        moved=16 * size,
        limit=WIDE_LIMIT,
    )(left, halo, clip, cot, weights, wpart, output)

    following = passed_along(head, "x", -1)
    input_grad = call(
        back_kernel,
        sds(frame, bf16),
        [VMEM, VMEM, VMEM, VMEM],
        HBM,
        scratch=[pltpu.VMEM(frame, bf16), dma((-(-count // 3),))],
        flops=count * 3 * work,
        moved=22 * size,
    )(grad, head, following, weights)

    terms = exchange(terms, ("c", "x"))
    half = sds((terms_shape[1] // 2, chans), f32)
    first, second = call(sum_kernel, (half, half), [VMEM], (VMEM, VMEM), moved=4 * size)(terms)
    first = lax.psum(first, ("z", "y"))
    second = lax.psum(second, ("y", "z"))
    terms = call(spread_kernel, sds(terms_shape, bf16), [VMEM, VMEM], VMEM, moved=4 * size)(first, second)
    terms = exchange(terms, ("c", "x"))
    weight_grad = small(last_kernel, terms, (3, chans, chans), f32)
    return (output[None], input_grad[None], weight_grad)


def solution(mesh):
    dp, tm = mesh.devices.shape
    side = math.isqrt(dp // 2)
    fine = Mesh(mesh.devices.reshape(side, -1, 2, tm), ("z", "y", "c", "x"))
    data = P(("z", "y", "c"), "x", None, None)
    in_specs = (P(("z", "y", "c")), data, P(), data)
    out_specs = (data, data, P())
    return jax.shard_map(local, mesh=fine, in_specs=in_specs, out_specs=out_specs, check_vma=False)
```

```python
import functools
import math

import jax
import jax.numpy as jnp
from jax import lax
from jax.experimental import pallas as pl
from jax.experimental.pallas import tpu as pltpu
from jax.sharding import Mesh, PartitionSpec as P

VMEM_LIMIT = 40 * 1024 * 1024
WIDE_LIMIT = 61 * 1024 * 1024
VMEM = pl.BlockSpec(memory_space=pltpu.VMEM)
SMEM = pl.BlockSpec(memory_space=pltpu.SMEM)
HBM = pl.BlockSpec(memory_space=pltpu.HBM)
ROWS = (((1,), (0,)), ((), ()))
COLS = (((1,), (1,)), ((), ()))


def dot(a, b, dims=ROWS):
    return lax.dot_general(a, b, dims, preferred_element_type=jnp.float32)


def activate(pre, cot, keep):
    sig = 0.5 * jnp.tanh(0.5 * pre) + 0.5
    value = keep * (pre * sig)
    slope = (keep * cot.astype(jnp.float32)) * (sig * (1.0 + pre * (1.0 - sig)))
    return value.astype(jnp.bfloat16), slope.astype(jnp.bfloat16)


def taps_of(frames, t, size):
    return jnp.concatenate([rows_of(frames[t - tap : t - tap + size]) for tap in range(3)], 1)


def rows_of(frames):
    return frames.reshape(-1, frames.shape[-1])


def body_kernel(
    left_ref, frames_hbm, cot_hbm, w_hbm, out_hbm, grad, wsum_ref,
    frames, cot, w, out, flipped, in_sem, cot_sem, w_sem, out_sem,
):
    count, pixels, width = frames.shape
    middle = 2 + (count - 2) // 2
    groups = [(2, middle), (middle, count)]
    copies = []
    for g, (start, end) in enumerate(groups):
        begin = 0 if g == 0 else start
        pair = []
        for source, target, sem, low in (
            (frames_hbm, frames, in_sem, begin), (cot_hbm, cot, cot_sem, start),
        ):
            part = pl.ds(low, end - low)
            pair.append(pltpu.make_async_copy(source.at[part], target.at[part], sem.at[g]))
        copies.append(pair)
    w_in = pltpu.make_async_copy(w_hbm, w, w_sem)
    copies[0][0].start()
    w_in.start()
    copies[0][1].start()
    copies[1][0].start()
    copies[1][1].start()
    copies[0][0].wait()
    w_in.wait()
    stacked = rows_of(w[...])
    pre = [dot(taps_of(frames, 2, middle - 2), stacked)]
    copies[0][1].wait()
    copies[1][0].wait()
    pre.append(dot(taps_of(frames, middle, count - middle), stacked))
    copies[1][1].wait()
    for t in range(count):
        flipped[:, t * pixels : (t + 1) * pixels] = frames[t].T
    total = None
    for g, (start, end) in enumerate(groups):
        slopes = []
        for t in range(start, end):
            rows = slice((t - start) * pixels, (t - start + 1) * pixels)
            keep = (t < left_ref[0]).astype(jnp.float32)
            value, slope = activate(pre[g][rows], cot[t], keep)
            out[t] = value
            grad[t] = slope
            slopes.append(slope)
        slope = jnp.concatenate(slopes, 0)
        for tap in range(3):
            term = dot(flipped[:, (start - tap) * pixels : (end - tap) * pixels], slope)
            part = slice(tap * width, (tap + 1) * width)
            wsum_ref[part, :] = term if g == 0 else wsum_ref[part, :] + term
    done = pltpu.make_async_copy(
        out.at[pl.ds(2, count - 2)], out_hbm.at[pl.ds(2, count - 2)], out_sem
    )
    done.start()
    done.wait()


def head_kernel(
    scale, left_ref, halo_hbm, frames_hbm, cot_hbm, w_hbm, wpart_hbm, out_in, out_hbm, head_ref, terms_ref,
    frames, cot, w, wpart, out, sems, out_sem,
):
    del out_in
    width = frames.shape[2]
    group = terms_ref.shape[0]
    share = width // group
    two = pl.ds(0, 2)
    copies = [
        pltpu.make_async_copy(source, target, sems.at[i])
        for i, (source, target) in enumerate(
            (
                (halo_hbm, frames.at[two]),
                (frames_hbm.at[two], frames.at[pl.ds(2, 2)]),
                (w_hbm, w),
                (cot_hbm.at[two], cot),
                (wpart_hbm, wpart),
            )
        )
    ]
    for copy in copies:
        copy.start()
    for copy in copies[:4]:
        copy.wait()
    pre = dot(taps_of(frames, 2, 2), rows_of(w[...]))
    flipped = [frames[t].T for t in range(4)]
    slopes = []
    for t in range(2):
        keep = (t < left_ref[0]).astype(jnp.float32)
        rows = slice(t * cot.shape[1], (t + 1) * cot.shape[1])
        value, slope = activate(pre[rows], cot[t], keep)
        out[t] = value
        head_ref[t] = slope
        slopes.append(slope)
    slope = jnp.concatenate(slopes, 0)
    out_copy = pltpu.make_async_copy(out, out_hbm.at[two], out_sem)
    out_copy.start()
    copies[4].wait()
    for tap in range(3):
        total = wpart[tap * width : (tap + 1) * width, :]
        total = total + dot(jnp.concatenate([flipped[2 - tap], flipped[3 - tap]], 1), slope)
        total = (total * scale).astype(jnp.bfloat16)
        for piece in range(group):
            terms_ref[piece, tap * share : (tap + 1) * share, :] = total[
                piece * share : (piece + 1) * share
            ]
    out_copy.wait()


def back_kernel(grad, head, halo, w, out_hbm, out, out_sem):
    count, pixels, width = out.shape
    weights = jnp.concatenate([w[tap].T for tap in range(3)], 0)
    size = 3
    for start in range(0, count, size):
        end = min(start + size, count)
        lines = []
        for tap in range(3):
            picked = []
            for t in range(start + tap, end + tap):
                picked.append(head[t] if t < 2 else grad[t] if t < count else halo[t - count])
            lines.append(jnp.concatenate(picked, 0))
        total = dot(jnp.concatenate(lines, 1), weights)
        out[start:end] = total.astype(jnp.bfloat16).reshape(end - start, pixels, width)
        part = pl.ds(start, end - start)
        pltpu.make_async_copy(out.at[part], out_hbm.at[part], out_sem.at[start // size]).start()
    for start in range(0, count, size):
        part = pl.ds(start, min(size, count - start))
        pltpu.make_async_copy(out.at[part], out_hbm.at[part], out_sem.at[start // size]).wait()


def cut_kernel(in_ref, out_ref):
    pieces, rows, cols = out_ref.shape
    across = in_ref.shape[1] // cols
    value = in_ref[...].astype(jnp.float32)
    for piece in range(pieces):
        r, h = divmod(piece, across)
        out_ref[piece] = value[r * rows : (r + 1) * rows, h * cols : (h + 1) * cols]


def sum_kernel(in_ref, out_ref):
    out_ref[...] = jnp.sum(in_ref[...], 0).astype(jnp.bfloat16)


def join_kernel(in_ref, out_ref):
    pieces, rows, cols = in_ref.shape
    across = out_ref.shape[1] // cols
    value = in_ref[...].astype(jnp.float32)
    for r in range(pieces // across):
        line = jnp.concatenate([value[r * across + h] for h in range(across)], 1)
        out_ref[r * rows : (r + 1) * rows, :] = line.astype(jnp.bfloat16)


def last_kernel(in_ref, out_ref):
    group = in_ref.shape[0]
    share = out_ref.shape[1] // group
    for piece in range(group):
        for tap in range(3):
            out_ref[tap, piece * share : (piece + 1) * share, :] = in_ref[
                piece, tap * share : (tap + 1) * share, :
            ].astype(jnp.float32)


def call(kernel, out_shape, in_specs, out_specs, scratch=(), aliases={}, flops=0, moved=0, limit=VMEM_LIMIT):
    return pl.pallas_call(
        kernel,
        out_shape=out_shape,
        in_specs=in_specs,
        out_specs=out_specs,
        scratch_shapes=list(scratch),
        input_output_aliases=aliases,
        compiler_params=pltpu.CompilerParams(vmem_limit_bytes=limit),
        cost_estimate=pl.CostEstimate(flops=flops, bytes_accessed=moved, transcendentals=0),
    )


def small(kernel, value, shape, dtype=jnp.bfloat16):
    return call(kernel, jax.ShapeDtypeStruct(shape, dtype), [VMEM], VMEM, moved=2 * value.size)(value)


def passed_along(value, axis, steps):
    count = lax.axis_size(axis)
    first, last = (max(0, -steps), min(count, count - steps))
    return lax.ppermute(value, axis, [(source, source + steps) for source in range(first, last)])


def local(lengths, frames, weights, cotangent):
    bf16, f32 = jnp.bfloat16, jnp.float32
    clip, cot = frames[0], cotangent[0]
    count, pixels, chans = clip.shape
    left = lengths - lax.axis_index("x") * count
    frame = (count, pixels, chans)
    sds = jax.ShapeDtypeStruct
    dma = pltpu.SemaphoreType.DMA
    halo = passed_along(clip[count - 2 :], "x", 1)
    size = pixels * chans * 2
    work = 2 * pixels * chans * chans
    output, grad, wpart = call(
        body_kernel,
        (sds(frame, bf16), sds(frame, bf16), sds((3 * chans, chans), f32)),
        [SMEM, HBM, HBM, HBM],
        (HBM, VMEM, VMEM),
        scratch=[
            pltpu.VMEM(frame, bf16),
            pltpu.VMEM(frame, bf16),
            pltpu.VMEM((3, chans, chans), bf16),
            pltpu.VMEM(frame, bf16),
            pltpu.VMEM((chans, count * pixels), bf16),
            dma((2,)),
            dma((2,)),
            dma,
            dma,
        ],
        flops=(count - 2) * 6 * work,
        moved=36 * size,
        limit=WIDE_LIMIT,
    )(left, clip, cot, weights)
    total_rows = lax.axis_size(("z", "y", "c", "x")) * count * pixels
    group = lax.axis_size(("c", "x"))
    terms_shape = (group, 3 * chans // group, chans)
    output, head, terms = call(
        functools.partial(head_kernel, 1.0 / math.sqrt(total_rows)),
        (sds(frame, bf16), sds((2, pixels, chans), bf16), sds(terms_shape, bf16)),
        [SMEM, HBM, HBM, HBM, HBM, HBM, HBM],
        (HBM, VMEM, VMEM),
        scratch=[
            pltpu.VMEM((4, pixels, chans), bf16),
            pltpu.VMEM((2, pixels, chans), bf16),
            pltpu.VMEM((3, chans, chans), bf16),
            pltpu.VMEM((3 * chans, chans), f32),
            pltpu.VMEM((2, pixels, chans), bf16),
            dma((5,)),
            dma,
        ],
        aliases={6: 0},
        flops=12 * work,
        moved=16 * size,
        limit=WIDE_LIMIT,
    )(left, halo, clip, cot, weights, wpart, output)

    following = passed_along(head, "x", -1)
    input_grad = call(
        back_kernel,
        sds(frame, bf16),
        [VMEM, VMEM, VMEM, VMEM],
        HBM,
        scratch=[pltpu.VMEM(frame, bf16), dma((-(-count // 3),))],
        flops=count * 3 * work,
        moved=22 * size,
    )(grad, head, following, weights)

    cols = 128
    rows = terms_shape[1] * chans // cols // lax.axis_size("y")
    terms = lax.psum_scatter(terms, ("c", "x"), scatter_dimension=0, tiled=False)
    terms = small(cut_kernel, terms, (lax.axis_size("y"), rows, cols), f32)
    terms = lax.psum_scatter(terms, "y", scatter_dimension=0, tiled=False)
    terms = lax.all_gather(terms, "z")
    terms = small(sum_kernel, terms, (rows, cols))
    terms = lax.all_gather(terms, "y")
    terms = small(join_kernel, terms, terms_shape[1:])
    terms = lax.all_gather(terms, ("c", "x"))
    weight_grad = small(last_kernel, terms, (3, chans, chans), f32)
    return (output[None], input_grad[None], weight_grad)


def solution(mesh):
    dp, tm = mesh.devices.shape
    side = math.isqrt(dp // 2)
    fine = Mesh(mesh.devices.reshape(side, -1, 2, tm), ("z", "y", "c", "x"))
    data = P(("z", "y", "c"), "x", None, None)
    in_specs = (P(("z", "y", "c")), data, P(), data)
    out_specs = (data, data, P())
    return jax.shard_map(local, mesh=fine, in_specs=in_specs, out_specs=out_specs, check_vma=False)
```

```python
import functools
import math

import jax
import jax.numpy as jnp
from jax import lax
from jax.experimental import pallas as pl
from jax.experimental.pallas import tpu as pltpu
from jax.sharding import Mesh, PartitionSpec as P

LANES = 128
HALVING = (("c", 1), ("x", 1), ("y", 1), ("z", 1), ("x", 2), ("y", 2))
DOUBLING = (("z", 2), ("y", 4), ("z", 4))
HEAD_ROUND = 5
VMEM_LIMIT = 40 * 1024 * 1024
WIDE_LIMIT = 61 * 1024 * 1024
VMEM = pl.BlockSpec(memory_space=pltpu.VMEM)
SMEM = pl.BlockSpec(memory_space=pltpu.SMEM)
HBM = pl.BlockSpec(memory_space=pltpu.HBM)
ROWS = (((1,), (0,)), ((), ()))
COLS = (((1,), (1,)), ((), ()))


def dot(a, b, dims=ROWS):
    return lax.dot_general(a, b, dims, preferred_element_type=jnp.float32)


def activate(pre, cot, keep):
    sig = 0.5 * jnp.tanh(0.5 * pre) + 0.5
    value = keep * (pre * sig)
    slope = (keep * cot.astype(jnp.float32)) * (sig * (1.0 + pre * (1.0 - sig)))
    return value.astype(jnp.bfloat16), slope.astype(jnp.bfloat16)


def taps_of(frames, t, size):
    return jnp.concatenate([rows_of(frames[t - tap : t - tap + size]) for tap in range(3)], 1)


def rows_of(frames):
    return frames.reshape(-1, frames.shape[-1])


def body_kernel(
    length_ref, frames_hbm, cot_hbm, w_hbm, out_hbm, grad, wsum_ref,
    frames, cot, w, out, flipped, in_sem, cot_sem, w_sem, out_sem,
):
    count, pixels, width = frames.shape
    middle = 2 + (count - 2) // 2
    groups = [(2, middle), (middle, count)]
    copies = []
    for g, (start, end) in enumerate(groups):
        begin = 0 if g == 0 else start
        pair = []
        for source, target, sem, low in (
            (frames_hbm, frames, in_sem, begin), (cot_hbm, cot, cot_sem, start),
        ):
            part = pl.ds(low, end - low)
            pair.append(pltpu.make_async_copy(source.at[part], target.at[part], sem.at[g]))
        copies.append(pair)
    w_in = pltpu.make_async_copy(w_hbm, w, w_sem)
    copies[0][0].start()
    w_in.start()
    copies[0][1].start()
    copies[1][0].start()
    copies[1][1].start()
    copies[0][0].wait()
    w_in.wait()
    stacked = rows_of(w[...])
    pre = [dot(taps_of(frames, 2, middle - 2), stacked)]
    copies[0][1].wait()
    copies[1][0].wait()
    pre.append(dot(taps_of(frames, middle, count - middle), stacked))
    copies[1][1].wait()
    for t in range(count):
        flipped[:, t * pixels : (t + 1) * pixels] = frames[t].T
    left = frames_left(length_ref, count)
    for g, (start, end) in enumerate(groups):
        slopes = []
        for t in range(start, end):
            rows = slice((t - start) * pixels, (t - start + 1) * pixels)
            keep = (t < left).astype(jnp.float32)
            value, slope = activate(pre[g][rows], cot[t], keep)
            out[t] = value
            grad[t] = slope
            slopes.append(slope)
        slope = jnp.concatenate(slopes, 0)
        for tap in range(3):
            term = dot(flipped[:, (start - tap) * pixels : (end - tap) * pixels], slope)
            part = slice(tap * width, (tap + 1) * width)
            wsum_ref[part, :] = term if g == 0 else wsum_ref[part, :] + term
    done = pltpu.make_async_copy(
        out.at[pl.ds(2, count - 2)], out_hbm.at[pl.ds(2, count - 2)], out_sem
    )
    done.start()
    done.wait()


def own_slot():
    me = jnp.int32(0)
    for axis, step in HALVING:
        if step < lax.axis_size(axis):
            me = 2 * me + lax.rem(lax.div(lax.axis_index(axis), step), 2)
    return me


def frames_left(length_ref, count):
    return length_ref[0] - lax.axis_index("x") * count


def piece_at(slot, me, rows):
    piece = lax.bitwise_xor(jnp.int32(slot), me)
    row = pl.multiple_of(lax.shift_right_logical(piece, 1) * rows, 8)
    col = pl.multiple_of(lax.bitwise_and(piece, 1) * LANES, LANES)
    return pl.ds(row, rows), pl.ds(col, LANES)


def head_kernel(
    scale, count, length_ref, halo_hbm, frames_hbm, cot_hbm, w_hbm, wpart_hbm, out_in,
    out_hbm, head_ref, keep_ref, send_ref,
    frames, cot, w, wpart, out, sems, out_sem,
):
    del out_in
    width = frames.shape[2]
    two = pl.ds(0, 2)
    copies = [
        pltpu.make_async_copy(source, target, sems.at[i])
        for i, (source, target) in enumerate(
            (
                (halo_hbm, frames.at[two]),
                (frames_hbm.at[two], frames.at[pl.ds(2, 2)]),
                (w_hbm, w),
                (cot_hbm.at[two], cot),
                (wpart_hbm, wpart),
            )
        )
    ]
    for copy in copies:
        copy.start()
    for copy in copies[:4]:
        copy.wait()
    left = frames_left(length_ref, count)
    me = own_slot()
    pre = dot(taps_of(frames, 2, 2), rows_of(w[...]))
    flipped = [frames[t].T for t in range(4)]
    slopes = []
    for t in range(2):
        keep = (t < left).astype(jnp.float32)
        rows = slice(t * cot.shape[1], (t + 1) * cot.shape[1])
        value, slope = activate(pre[rows], cot[t], keep)
        out[t] = value
        head_ref[t] = slope
        slopes.append(slope)
    slope = jnp.concatenate(slopes, 0)
    out_copy = pltpu.make_async_copy(out, out_hbm.at[two], out_sem)
    out_copy.start()
    copies[4].wait()
    for tap in range(3):
        part = slice(tap * width, (tap + 1) * width)
        term = dot(jnp.concatenate([flipped[2 - tap], flipped[3 - tap]], 1), slope)
        wpart[part, :] = (wpart[part, :] + term) * scale
    half, rows, _ = keep_ref.shape
    for slot in range(2 * half):
        value = wpart[piece_at(slot, me, rows)]
        if slot < half:
            keep_ref[slot] = value
        else:
            send_ref[slot - half] = value.astype(jnp.bfloat16)
    out_copy.wait()


def back_kernel(grad, head, halo, w, out_hbm, out, out_sem):
    count, pixels, width = out.shape
    weights = jnp.concatenate([w[tap].T for tap in range(3)], 0)
    size = 3
    for start in range(0, count, size):
        end = min(start + size, count)
        lines = []
        for tap in range(3):
            picked = []
            for t in range(start + tap, end + tap):
                picked.append(head[t] if t < 2 else grad[t] if t < count else halo[t - count])
            lines.append(jnp.concatenate(picked, 0))
        total = dot(jnp.concatenate(lines, 1), weights)
        out[start:end] = total.astype(jnp.bfloat16).reshape(end - start, pixels, width)
        part = pl.ds(start, end - start)
        pltpu.make_async_copy(out.at[part], out_hbm.at[part], out_sem.at[start // size]).start()
    for start in range(0, count, size):
        part = pl.ds(start, min(size, count - start))
        pltpu.make_async_copy(out.at[part], out_hbm.at[part], out_sem.at[start // size]).wait()


def halve_kernel(kept_ref, got_ref, *refs):
    keep_ref, send_ref = refs[-2:]
    half = keep_ref.shape[0]
    keep_ref[...] = kept_ref[:half] + got_ref[:half].astype(jnp.float32)
    send_ref[...] = (kept_ref[half:] + got_ref[half:].astype(jnp.float32)).astype(jnp.bfloat16)


def add_kernel(kept_ref, got_ref, out_ref):
    total = kept_ref[...] + got_ref[...].astype(jnp.float32)
    out_ref[...] = total.astype(out_ref.dtype)


def join_kernel(kept_ref, got_ref, out_ref):
    half = kept_ref.shape[0]
    out_ref[:half] = kept_ref[...]
    out_ref[half:] = got_ref[...]


def last_kernel(kept_ref, got_ref, out_ref):
    half, rows, _ = kept_ref.shape
    me = own_slot()
    for slot in range(2 * half):
        value = kept_ref[slot] if slot < half else got_ref[slot - half]
        out_ref[piece_at(slot, me, rows)] = value.astype(jnp.float32)


def call(kernel, out_shape, in_specs, out_specs, scratch=(), aliases={}, flops=0, moved=0, limit=VMEM_LIMIT):
    return pl.pallas_call(
        kernel,
        out_shape=out_shape,
        in_specs=in_specs,
        out_specs=out_specs,
        scratch_shapes=list(scratch),
        input_output_aliases=aliases,
        compiler_params=pltpu.CompilerParams(vmem_limit_bytes=limit),
        cost_estimate=pl.CostEstimate(flops=flops, bytes_accessed=moved, transcendentals=0),
    )


def passed_along(value, axis, steps):
    count = lax.axis_size(axis)
    first, last = (max(0, -steps), min(count, count - steps))
    return lax.ppermute(value, axis, [(source, source + steps) for source in range(first, last)])


def swapped(value, axis, step):
    return lax.ppermute(value, axis, [(i, i ^ step) for i in range(lax.axis_size(axis))])


def local(lengths, frames, weights, cotangent):
    bf16, f32 = jnp.bfloat16, jnp.float32
    clip, cot = frames[0], cotangent[0]
    count, pixels, chans = clip.shape
    frame = (count, pixels, chans)
    sds = jax.ShapeDtypeStruct
    dma = pltpu.SemaphoreType.DMA
    halving = [(axis, step) for axis, step in HALVING if step < lax.axis_size(axis)]
    doubling = [(axis, step) for axis, step in DOUBLING if step < lax.axis_size(axis)]
    halo = passed_along(clip[count - 2 :], "x", 1)
    size = pixels * chans * 2
    work = 2 * pixels * chans * chans
    output, grad, wpart = call(
        body_kernel,
        (sds(frame, bf16), sds(frame, bf16), sds((3 * chans, chans), f32)),
        [SMEM, HBM, HBM, HBM],
        (HBM, VMEM, VMEM),
        scratch=[
            pltpu.VMEM(frame, bf16),
            pltpu.VMEM(frame, bf16),
            pltpu.VMEM((3, chans, chans), bf16),
            pltpu.VMEM(frame, bf16),
            pltpu.VMEM((chans, count * pixels), bf16),
            dma((2,)),
            dma((2,)),
            dma,
            dma,
        ],
        flops=(count - 2) * 6 * work,
        moved=36 * size,
        limit=WIDE_LIMIT,
    )(lengths, clip, cot, weights)
    total_rows = lax.axis_size(("z", "y", "c", "x")) * count * pixels
    half = 2 ** (len(halving) - 1)
    piece = (3 * chans * chans // LANES // (2 * half), LANES)
    output, head, keep, send = call(
        functools.partial(head_kernel, 1.0 / math.sqrt(total_rows), count),
        (
            sds(frame, bf16),
            sds((2, pixels, chans), bf16),
            sds((half,) + piece, f32),
            sds((half,) + piece, bf16),
        ),
        [SMEM, HBM, HBM, HBM, HBM, HBM, HBM],
        (HBM, VMEM, VMEM, VMEM),
        scratch=[
            pltpu.VMEM((4, pixels, chans), bf16),
            pltpu.VMEM((2, pixels, chans), bf16),
            pltpu.VMEM((3, chans, chans), bf16),
            pltpu.VMEM((3 * chans, chans), f32),
            pltpu.VMEM((2, pixels, chans), bf16),
            dma((5,)),
            dma,
        ],
        aliases={6: 0},
        flops=12 * work,
        moved=16 * size,
        limit=WIDE_LIMIT,
    )(lengths, halo, clip, cot, weights, wpart, output)

    for number, (axis, step) in enumerate(halving[:-1]):
        got = swapped(send, axis, step)
        half //= 2
        shapes = [sds((half,) + piece, f32), sds((half,) + piece, bf16)]
        if number + 1 == HEAD_ROUND:
            head, keep, send = call(
                halve_kernel, [sds(head.shape, bf16)] + shapes, [VMEM, VMEM, HBM], [HBM, VMEM, VMEM],
                aliases={2: 0},
            )(keep, got, head)
        else:
            keep, send = call(halve_kernel, shapes, [VMEM, VMEM], [VMEM, VMEM])(keep, got)
    rounds = halving[-1:] + doubling
    for number, (axis, step) in enumerate(rounds):
        got = swapped(send, axis, step)
        dtype = bf16 if number == len(rounds) - 1 else f32
        keep = send = call(add_kernel, sds((1,) + piece, dtype), [VMEM, VMEM], VMEM)(keep, got)
    following = passed_along(head, "x", -1)
    input_grad = call(
        back_kernel,
        sds(frame, bf16),
        [VMEM, VMEM, VMEM, VMEM],
        HBM,
        scratch=[pltpu.VMEM(frame, bf16), dma((-(-count // 3),))],
        flops=count * 3 * work,
        moved=22 * size,
    )(grad, head, following, weights)
    for axis, step in halving[:0:-1]:
        got = swapped(keep, axis, step)
        keep = call(join_kernel, sds((2 * keep.shape[0],) + piece, bf16), [VMEM, VMEM], VMEM)(keep, got)
    got = swapped(keep, *halving[0])
    weight_grad = call(last_kernel, sds((3 * chans, chans), f32), [VMEM, VMEM], VMEM)(keep, got)
    return (output[None], input_grad[None], weight_grad.reshape(3, chans, chans))


def solution(mesh):
    dp, tm = mesh.devices.shape
    side = math.isqrt(dp // 2)
    fine = Mesh(mesh.devices.reshape(side, -1, 2, tm), ("z", "y", "c", "x"))
    data = P(("z", "y", "c"), "x", None, None)
    in_specs = (P(("z", "y", "c")), data, P(), data)
    out_specs = (data, data, P())
    return jax.shard_map(local, mesh=fine, in_specs=in_specs, out_specs=out_specs, check_vma=False)
```

```python
import functools
import math

import jax
import jax.numpy as jnp
from jax import lax
from jax.experimental import pallas as pl
from jax.experimental.pallas import tpu as pltpu
from jax.sharding import Mesh, PartitionSpec as P

LANES = 128
MESH_AXES = ("z", "far_y", "y", "c", "x")
SCATTER = ("c", "x", "y")
SUM = ("z", "far_y")
NEAR_Y = 4
VMEM_LIMIT = 40 * 1024 * 1024
WIDE_LIMIT = 61 * 1024 * 1024
VMEM = pl.BlockSpec(memory_space=pltpu.VMEM)
SMEM = pl.BlockSpec(memory_space=pltpu.SMEM)
HBM = pl.BlockSpec(memory_space=pltpu.HBM)
ROWS = (((1,), (0,)), ((), ()))
COLS = (((1,), (1,)), ((), ()))


def dot(a, b, dims=ROWS):
    return lax.dot_general(a, b, dims, preferred_element_type=jnp.float32)


def activate(pre, cot, keep):
    sig = 0.5 * jnp.tanh(0.5 * pre) + 0.5
    value = keep * (pre * sig)
    slope = (keep * cot.astype(jnp.float32)) * (sig * (1.0 + pre * (1.0 - sig)))
    return value.astype(jnp.bfloat16), slope.astype(jnp.bfloat16)


def taps_of(frames, t, size):
    return jnp.concatenate([rows_of(frames[t - tap : t - tap + size]) for tap in range(3)], 1)


def rows_of(frames):
    return frames.reshape(-1, frames.shape[-1])


def body_kernel(
    length_ref, frames_hbm, cot_hbm, w_hbm, out_hbm, grad, wsum_ref, first_ref,
    frames, cot, w, out, flipped, in_sem, cot_sem, w_sem, out_sem,
):
    count, pixels, width = frames.shape
    middle = 2 + (count - 2) // 2
    groups = [(2, middle), (middle, count)]
    copies = []
    for g, (start, end) in enumerate(groups):
        part = pl.ds(0 if g == 0 else start, end if g == 0 else end - start)
        pair = []
        for source, target, sem in ((frames_hbm, frames, in_sem), (cot_hbm, cot, cot_sem)):
            pair.append(pltpu.make_async_copy(source.at[part], target.at[part], sem.at[g]))
        copies.append(pair)
    w_in = pltpu.make_async_copy(w_hbm, w, w_sem)
    copies[0][0].start()
    w_in.start()
    copies[0][1].start()
    copies[1][0].start()
    copies[1][1].start()
    copies[0][0].wait()
    w_in.wait()
    stacked = rows_of(w[...])
    pre = [dot(taps_of(frames, 2, middle - 2), stacked)]
    copies[0][1].wait()
    copies[1][0].wait()
    pre.append(dot(taps_of(frames, middle, count - middle), stacked))
    copies[1][1].wait()
    for t in range(count):
        flipped[:, t * pixels : (t + 1) * pixels] = frames[t].T
    left = frames_left(length_ref, count)
    done = []
    for g, (start, end) in enumerate(groups):
        slopes = []
        for t in range(start, end):
            rows = slice((t - start) * pixels, (t - start + 1) * pixels)
            keep = (t < left).astype(jnp.float32)
            value, slope = activate(pre[g][rows], cot[t], keep)
            out[t] = value
            grad[t] = slope
            slopes.append(slope)
        part = pl.ds(start, end - start)
        done.append(pltpu.make_async_copy(out.at[part], out_hbm.at[part], out_sem.at[g]))
        done[-1].start()
        slope = jnp.concatenate(slopes, 0)
        for tap in range(3):
            term = dot(flipped[:, (start - tap) * pixels : (end - tap) * pixels], slope)
            part = slice(tap * width, (tap + 1) * width)
            wsum_ref[part, :] = term if g == 0 else wsum_ref[part, :] + term
    first_ref[:2] = frames[:2]
    first_ref[2:] = cot[:2]
    for copy in done:
        copy.wait()


def frames_left(length_ref, count):
    return length_ref[0] - lax.axis_index("x") * count


def piece_at(piece, rows):
    row, col = divmod(piece, 2)
    return slice(row * rows, (row + 1) * rows), slice(col * LANES, (col + 1) * LANES)


def head_kernel(
    scale, count, length_ref, halo, first, w, wpart, out_in, out_hbm, head_ref, terms_ref,
    out, total, out_sem,
):
    del out_in
    pixels, width = halo.shape[1:]
    left = frames_left(length_ref, count)
    back = [halo[0], halo[1], first[0], first[1]]
    lines = [jnp.concatenate(back[2 - tap : 4 - tap], 0) for tap in range(3)]
    pre = dot(jnp.concatenate(lines, 1), rows_of(w[...]))
    flipped = [frame.T for frame in back]
    slopes = []
    for t in range(2):
        keep = (t < left).astype(jnp.float32)
        value, slope = activate(pre[t * pixels : (t + 1) * pixels], first[2 + t], keep)
        out[t] = value
        head_ref[t] = slope
        slopes.append(slope)
    slope = jnp.concatenate(slopes, 0)
    out_copy = pltpu.make_async_copy(out, out_hbm.at[pl.ds(0, 2)], out_sem)
    out_copy.start()
    for tap in range(3):
        part = slice(tap * width, (tap + 1) * width)
        term = dot(jnp.concatenate([flipped[2 - tap], flipped[3 - tap]], 1), slope)
        total[part, :] = (wpart[part, :] + term) * scale
    pieces, rows, _ = terms_ref.shape
    for piece in range(pieces):
        terms_ref[piece] = total[piece_at(piece, rows)].astype(jnp.bfloat16)
    out_copy.wait()


def back_kernel(grad, head, halo, w, out_hbm, out, out_sem):
    count, pixels, width = out.shape
    weights = jnp.concatenate([w[tap].T for tap in range(3)], 0)
    size = 3
    for start in range(0, count, size):
        end = min(start + size, count)
        lines = []
        for tap in range(3):
            picked = []
            for t in range(start + tap, end + tap):
                picked.append(head[t] if t < 2 else grad[t] if t < count else halo[t - count])
            lines.append(jnp.concatenate(picked, 0))
        total = dot(jnp.concatenate(lines, 1), weights)
        out[start:end] = total.astype(jnp.bfloat16).reshape(end - start, pixels, width)
        part = pl.ds(start, end - start)
        pltpu.make_async_copy(out.at[part], out_hbm.at[part], out_sem.at[start // size]).start()
    for start in range(0, count, size):
        part = pl.ds(start, min(size, count - start))
        pltpu.make_async_copy(out.at[part], out_hbm.at[part], out_sem.at[start // size]).wait()


def spread_sum_kernel(in_ref, passed_in, out_ref, passed_out):
    del passed_in, passed_out
    total = jnp.sum(in_ref[...].astype(jnp.float32), 0).astype(jnp.bfloat16)
    for piece in range(out_ref.shape[0]):
        out_ref[piece] = total


def last_kernel(in_ref, out_ref):
    pieces, rows, _ = in_ref.shape
    for piece in range(pieces):
        out_ref[piece_at(piece, rows)] = in_ref[piece].astype(jnp.float32)


def call(kernel, out_shape, in_specs, out_specs, scratch=(), aliases={}, flops=0, moved=0, limit=VMEM_LIMIT):
    return pl.pallas_call(
        kernel,
        out_shape=out_shape,
        in_specs=in_specs,
        out_specs=out_specs,
        scratch_shapes=list(scratch),
        input_output_aliases=aliases,
        compiler_params=pltpu.CompilerParams(vmem_limit_bytes=limit),
        cost_estimate=pl.CostEstimate(flops=flops, bytes_accessed=moved, transcendentals=0),
    )


def passed_along(value, axis, steps):
    count = lax.axis_size(axis)
    first, last = (max(0, -steps), min(count, count - steps))
    return lax.ppermute(value, axis, [(source, source + steps) for source in range(first, last)])


def exchange(value, axes):
    return lax.all_to_all(value, axes, 0, 0, tiled=True)


def spread_sum(terms, passed, copies):
    sds = jax.ShapeDtypeStruct
    shapes = (sds((copies,) + terms.shape[1:], terms.dtype), sds(passed.shape, passed.dtype))
    anywhere = pl.BlockSpec(memory_space=pl.ANY)
    return call(spread_sum_kernel, shapes, [VMEM, anywhere], (VMEM, anywhere), aliases={1: 1})(terms, passed)


def local(lengths, frames, weights, cotangent):
    bf16, f32 = jnp.bfloat16, jnp.float32
    clip, cot = frames[0], cotangent[0]
    count, pixels, chans = clip.shape
    frame = (count, pixels, chans)
    sds = jax.ShapeDtypeStruct
    dma = pltpu.SemaphoreType.DMA
    halo = passed_along(clip[count - 2 :], "x", 1)
    size = pixels * chans * 2
    work = 2 * pixels * chans * chans
    output, grad, wpart, first = call(
        body_kernel,
        (sds(frame, bf16), sds(frame, bf16), sds((3 * chans, chans), f32), sds((4, pixels, chans), bf16)),
        [SMEM, HBM, HBM, HBM],
        (HBM, VMEM, VMEM, VMEM),
        scratch=[
            pltpu.VMEM(frame, bf16),
            pltpu.VMEM(frame, bf16),
            pltpu.VMEM((3, chans, chans), bf16),
            pltpu.VMEM(frame, bf16),
            pltpu.VMEM((chans, count * pixels), bf16),
            dma((2,)),
            dma((2,)),
            dma,
            dma((2,)),
        ],
        flops=(count - 2) * 6 * work,
        moved=36 * size,
        limit=WIDE_LIMIT,
    )(lengths, clip, cot, weights)
    total_rows = lax.axis_size(MESH_AXES) * count * pixels
    pieces, terms_of = lax.axis_size(SCATTER), lax.axis_size(SUM)
    output, head, terms = call(
        functools.partial(head_kernel, 1.0 / math.sqrt(total_rows), count),
        (
            sds(frame, bf16),
            sds((2, pixels, chans), bf16),
            sds((pieces, 3 * chans * chans // LANES // pieces, LANES), bf16),
        ),
        [SMEM, VMEM, VMEM, VMEM, VMEM, HBM],
        (HBM, VMEM, VMEM),
        scratch=[
            pltpu.VMEM((2, pixels, chans), bf16),
            pltpu.VMEM((3 * chans, chans), f32),
            dma,
        ],
        aliases={5: 0},
        flops=12 * work,
        moved=16 * size,
    )(lengths, halo, first, weights, wpart, output)

    terms, head = spread_sum(exchange(terms, SCATTER), head, terms_of)
    following = passed_along(head, "x", -1)
    terms, following = spread_sum(exchange(terms, SUM), following, pieces)
    terms = exchange(terms, SCATTER)
    input_grad = call(
        back_kernel,
        sds(frame, bf16),
        [VMEM, VMEM, VMEM, VMEM],
        HBM,
        scratch=[pltpu.VMEM(frame, bf16), dma((-(-count // 3),))],
        flops=count * 3 * work,
        moved=22 * size,
    )(grad, head, following, weights)
    weight_grad = call(last_kernel, sds((3 * chans, chans), f32), [VMEM], VMEM)(terms)
    return (output[None], input_grad[None], weight_grad.reshape(3, chans, chans))


def solution(mesh):
    dp, tm = mesh.devices.shape
    side = math.isqrt(dp // 2)
    fine = Mesh(mesh.devices.reshape(side, side // NEAR_Y, NEAR_Y, 2, tm), MESH_AXES)
    data = P(MESH_AXES[:4], "x", None, None)
    in_specs = (P(MESH_AXES[:4]), data, P(), data)
    out_specs = (data, data, P())
    return jax.shard_map(local, mesh=fine, in_specs=in_specs, out_specs=out_specs, check_vma=False)
```

```python
import functools
import math

import jax
import jax.numpy as jnp
from jax import lax
from jax.experimental import pallas as pl
from jax.experimental.pallas import tpu as pltpu
from jax.sharding import Mesh, PartitionSpec as P

LANES = 128
MESH_AXES = ("far_z", "z", "far_y", "y", "c", "x")
SCATTER = ("c", "x", "y", "z")
SUM = ("far_z", "far_y")
VMEM_LIMIT = 40 * 1024 * 1024
VMEM = pl.BlockSpec(memory_space=pltpu.VMEM)
SMEM = pl.BlockSpec(memory_space=pltpu.SMEM)
HBM = pl.BlockSpec(memory_space=pltpu.HBM)
ROWS = (((1,), (0,)), ((), ()))
COLS = (((1,), (1,)), ((), ()))


def dot(a, b, dims=ROWS):
    return lax.dot_general(a, b, dims, preferred_element_type=jnp.float32)


def activate(pre, cot, keep):
    sig = 0.5 * jnp.tanh(0.5 * pre) + 0.5
    value = keep * (pre * sig)
    slope = (keep * cot.astype(jnp.float32)) * (sig * (1.0 + pre * (1.0 - sig)))
    return value.astype(jnp.bfloat16), slope.astype(jnp.bfloat16)


def taps_of(frames, t, size):
    return jnp.concatenate([rows_of(frames[t - tap : t - tap + size]) for tap in range(3)], 1)


def rows_of(frames):
    return frames.reshape(-1, frames.shape[-1])


def body_kernel(length_ref, frames, cot, w, out_hbm, grad, wsum_ref, out, flipped, out_sem):
    count, pixels, width = frames.shape
    middle = 2 + (count - 2) // 2
    groups = [(2, middle), (middle, count)]
    stacked = rows_of(w[...])
    pre = [dot(taps_of(frames, 2, middle - 2), stacked)]
    pre.append(dot(taps_of(frames, middle, count - middle), stacked))
    for t in range(count):
        flipped[:, t * pixels : (t + 1) * pixels] = frames[t].T
    left = frames_left(length_ref, count)
    done = []
    for g, (start, end) in enumerate(groups):
        slopes = []
        for t in range(start, end):
            rows = slice((t - start) * pixels, (t - start + 1) * pixels)
            keep = (t < left).astype(jnp.float32)
            value, slope = activate(pre[g][rows], cot[t], keep)
            out[t] = value
            grad[t] = slope
            slopes.append(slope)
        part = pl.ds(start, end - start)
        done.append(pltpu.make_async_copy(out.at[part], out_hbm.at[part], out_sem.at[g]))
        done[-1].start()
        slope = jnp.concatenate(slopes, 0)
        for tap in range(3):
            term = dot(flipped[:, (start - tap) * pixels : (end - tap) * pixels], slope)
            part = slice(tap * width, (tap + 1) * width)
            wsum_ref[part, :] = term if g == 0 else wsum_ref[part, :] + term
    for copy in done:
        copy.wait()


def frames_left(length_ref, count):
    return length_ref[0] - lax.axis_index("x") * count


def piece_at(piece, rows):
    row, col = divmod(piece, 2)
    return slice(row * rows, (row + 1) * rows), slice(col * LANES, (col + 1) * LANES)


def head_kernel(
    scale, count, length_ref, halo, frames, cot, w, wpart, out_in, out_hbm, head_ref, terms_ref,
    out, total, out_sem,
):
    del out_in
    pixels, width = halo.shape[1:]
    left = frames_left(length_ref, count)
    back = [halo[0], halo[1], frames[0], frames[1]]
    lines = [jnp.concatenate(back[2 - tap : 4 - tap], 0) for tap in range(3)]
    pre = dot(jnp.concatenate(lines, 1), rows_of(w[...]))
    flipped = [frame.T for frame in back]
    slopes = []
    for t in range(2):
        keep = (t < left).astype(jnp.float32)
        value, slope = activate(pre[t * pixels : (t + 1) * pixels], cot[t], keep)
        out[t] = value
        head_ref[t] = slope
        slopes.append(slope)
    slope = jnp.concatenate(slopes, 0)
    out_copy = pltpu.make_async_copy(out, out_hbm.at[pl.ds(0, 2)], out_sem)
    out_copy.start()
    for tap in range(3):
        part = slice(tap * width, (tap + 1) * width)
        term = dot(jnp.concatenate([flipped[2 - tap], flipped[3 - tap]], 1), slope)
        total[part, :] = (wpart[part, :] + term) * scale
    pieces, rows, _ = terms_ref.shape
    for piece in range(pieces):
        terms_ref[piece] = total[piece_at(piece, rows)].astype(jnp.bfloat16)
    out_copy.wait()


def back_kernel(grad, head, halo, w, out_hbm, out, out_sem):
    count, pixels, width = out.shape
    weights = jnp.concatenate([w[tap].T for tap in range(3)], 0)
    size = 3
    for start in range(0, count, size):
        end = min(start + size, count)
        lines = []
        for tap in range(3):
            picked = []
            for t in range(start + tap, end + tap):
                picked.append(head[t] if t < 2 else grad[t] if t < count else halo[t - count])
            lines.append(jnp.concatenate(picked, 0))
        total = dot(jnp.concatenate(lines, 1), weights)
        out[start:end] = total.astype(jnp.bfloat16).reshape(end - start, pixels, width)
        part = pl.ds(start, end - start)
        pltpu.make_async_copy(out.at[part], out_hbm.at[part], out_sem.at[start // size]).start()
    for start in range(0, count, size):
        part = pl.ds(start, min(size, count - start))
        pltpu.make_async_copy(out.at[part], out_hbm.at[part], out_sem.at[start // size]).wait()


def spread_sum_kernel(in_ref, *refs):
    out_ref = refs[-1]
    total = jnp.sum(in_ref[...].astype(jnp.float32), 0).astype(jnp.bfloat16)
    for piece in range(out_ref.shape[0]):
        out_ref[piece] = total


def last_kernel(in_ref, out_ref):
    pieces, rows, _ = in_ref.shape
    for piece in range(pieces):
        out_ref[piece_at(piece, rows)] = in_ref[piece].astype(jnp.float32)


def call(kernel, out_shape, in_specs, out_specs, scratch=(), aliases={}, flops=0, moved=0):
    return pl.pallas_call(
        kernel,
        out_shape=out_shape,
        in_specs=in_specs,
        out_specs=out_specs,
        scratch_shapes=list(scratch),
        input_output_aliases=aliases,
        compiler_params=pltpu.CompilerParams(vmem_limit_bytes=VMEM_LIMIT),
        cost_estimate=pl.CostEstimate(flops=flops, bytes_accessed=moved, transcendentals=0),
    )


def passed_along(value, axis, steps):
    count = lax.axis_size(axis)
    first, last = (max(0, -steps), min(count, count - steps))
    return lax.ppermute(value, axis, [(source, source + steps) for source in range(first, last)])


def exchange(value, axes):
    return lax.all_to_all(value, axes, 0, 0, tiled=True)


def spread_sum(terms, copies, *passed):
    sds = jax.ShapeDtypeStruct
    shapes = [sds(value.shape, value.dtype) for value in passed]
    shapes.append(sds((copies,) + terms.shape[1:], terms.dtype))
    anywhere = [pl.BlockSpec(memory_space=pl.ANY)] * len(passed)
    aliases = {i + 1: i for i in range(len(passed))}
    return call(spread_sum_kernel, shapes, [VMEM] + anywhere, anywhere + [VMEM], aliases=aliases)(
        terms, *passed
    )


def local(lengths, frames, weights, cotangent):
    bf16, f32 = jnp.bfloat16, jnp.float32
    clip, cot = frames[0], cotangent[0]
    count, pixels, chans = clip.shape
    frame = (count, pixels, chans)
    sds = jax.ShapeDtypeStruct
    dma = pltpu.SemaphoreType.DMA
    halo = passed_along(clip[count - 2 :], "x", 1)
    size = pixels * chans * 2
    work = 2 * pixels * chans * chans
    output, grad, wpart = call(
        body_kernel,
        (sds(frame, bf16), sds(frame, bf16), sds((3 * chans, chans), f32)),
        [SMEM, VMEM, VMEM, VMEM],
        (HBM, VMEM, VMEM),
        scratch=[pltpu.VMEM(frame, bf16), pltpu.VMEM((chans, count * pixels), bf16), dma((2,))],
        flops=(count - 2) * 6 * work,
        moved=36 * size,
    )(lengths, clip, cot, weights)
    total_rows = lax.axis_size(MESH_AXES) * count * pixels
    pieces, terms_of = lax.axis_size(SCATTER), lax.axis_size(SUM)
    output, head, terms = call(
        functools.partial(head_kernel, 1.0 / math.sqrt(total_rows), count),
        (
            sds(frame, bf16),
            sds((2, pixels, chans), bf16),
            sds((pieces, 3 * chans * chans // LANES // pieces, LANES), bf16),
        ),
        [SMEM, VMEM, VMEM, VMEM, VMEM, VMEM, HBM],
        (HBM, VMEM, VMEM),
        scratch=[
            pltpu.VMEM((2, pixels, chans), bf16),
            pltpu.VMEM((3 * chans, chans), f32),
            dma,
        ],
        aliases={6: 0},
        flops=12 * work,
        moved=16 * size,
    )(lengths, halo, clip, cot, weights, wpart, output)

    head, terms = spread_sum(exchange(terms, SCATTER), terms_of, head)
    following = passed_along(head, "x", -1)
    (terms,) = spread_sum(exchange(terms, SUM), pieces)
    terms = exchange(terms, SCATTER)
    input_grad = call(
        back_kernel,
        sds(frame, bf16),
        [VMEM, VMEM, VMEM, VMEM],
        HBM,
        scratch=[pltpu.VMEM(frame, bf16), dma((-(-count // 3),))],
        flops=count * 3 * work,
        moved=22 * size,
    )(grad, head, following, weights)
    weight_grad = call(last_kernel, sds((3 * chans, chans), f32), [VMEM], VMEM)(terms)
    return (output[None], input_grad[None], weight_grad.reshape(3, chans, chans))


def solution(mesh):
    dp, tm = mesh.devices.shape
    side = math.isqrt(dp // 2)
    fine = Mesh(mesh.devices.reshape(side // 2, 2, -1, 2, 2, tm), MESH_AXES)
    data = P(MESH_AXES[:5], "x", None, None)
    in_specs = (P(MESH_AXES[:5]), data, P(), data)
    out_specs = (data, data, P())
    return jax.shard_map(local, mesh=fine, in_specs=in_specs, out_specs=out_specs, check_vma=False)
```

```python
import functools
import math

import jax
import jax.numpy as jnp
from jax import lax
from jax.experimental import pallas as pl
from jax.experimental.pallas import tpu as pltpu
from jax.sharding import Mesh, PartitionSpec as P

LANES = 128
MESH_AXES = ("far_z", "z", "far_y", "y", "c", "x")
SCATTER = ("c", "x", "y", "z")
SUM = ("far_z", "far_y")
VMEM_LIMIT = 40 * 1024 * 1024
VMEM = pl.BlockSpec(memory_space=pltpu.VMEM)
SMEM = pl.BlockSpec(memory_space=pltpu.SMEM)
HBM = pl.BlockSpec(memory_space=pltpu.HBM)
ROWS = (((1,), (0,)), ((), ()))
COLS = (((1,), (1,)), ((), ()))


def dot(a, b, dims=ROWS):
    return lax.dot_general(a, b, dims, preferred_element_type=jnp.float32)


def activate(pre, cot, keep):
    sig = 0.5 * jnp.tanh(0.5 * pre) + 0.5
    value = keep * (pre * sig)
    slope = (keep * cot.astype(jnp.float32)) * (sig * (1.0 + pre * (1.0 - sig)))
    return value.astype(jnp.bfloat16), slope.astype(jnp.bfloat16)


def taps_of(frames, t, size):
    return jnp.concatenate([rows_of(frames[t - tap : t - tap + size]) for tap in range(3)], 1)


def rows_of(frames):
    return frames.reshape(-1, frames.shape[-1])


def body_kernel(length_ref, frames, cot, w, out_hbm, grad, wsum_ref, out, flipped, out_sem):
    count, pixels, width = frames.shape
    middle = 2 + (count - 2) // 2
    groups = [(2, middle), (middle, count)]
    stacked = rows_of(w[...])
    pre = [dot(taps_of(frames, 2, middle - 2), stacked)]
    pre.append(dot(taps_of(frames, middle, count - middle), stacked))
    for t in range(count):
        flipped[:, t * pixels : (t + 1) * pixels] = frames[t].T
    left = frames_left(length_ref, count)
    done = []
    for g, (start, end) in enumerate(groups):
        slopes = []
        for t in range(start, end):
            rows = slice((t - start) * pixels, (t - start + 1) * pixels)
            keep = (t < left).astype(jnp.float32)
            value, slope = activate(pre[g][rows], cot[t], keep)
            out[t] = value
            grad[t] = slope
            slopes.append(slope)
        part = pl.ds(start, end - start)
        done.append(pltpu.make_async_copy(out.at[part], out_hbm.at[part], out_sem.at[g]))
        done[-1].start()
        slope = jnp.concatenate(slopes, 0)
        for tap in range(3):
            term = dot(flipped[:, (start - tap) * pixels : (end - tap) * pixels], slope)
            part = slice(tap * width, (tap + 1) * width)
            wsum_ref[part, :] = term if g == 0 else wsum_ref[part, :] + term
    for copy in done:
        copy.wait()


def frames_left(length_ref, count):
    return length_ref[0] - lax.axis_index("x") * count


def piece_at(piece, rows):
    row, col = divmod(piece, 2)
    return slice(row * rows, (row + 1) * rows), slice(col * LANES, (col + 1) * LANES)


def head_kernel(
    scale, count, length_ref, halo, frames, cot, w, wpart, out_in, out_hbm, head_ref, terms_ref,
    out, total, out_sem,
):
    del out_in
    pixels, width = halo.shape[1:]
    left = frames_left(length_ref, count)
    back = [halo[0], halo[1], frames[0], frames[1]]
    lines = [jnp.concatenate(back[2 - tap : 4 - tap], 0) for tap in range(3)]
    pre = dot(jnp.concatenate(lines, 1), rows_of(w[...]))
    flipped = [frame.T for frame in back]
    slopes = []
    for t in range(2):
        keep = (t < left).astype(jnp.float32)
        value, slope = activate(pre[t * pixels : (t + 1) * pixels], cot[t], keep)
        out[t] = value
        head_ref[t] = slope
        slopes.append(slope)
    slope = jnp.concatenate(slopes, 0)
    out_copy = pltpu.make_async_copy(out, out_hbm.at[pl.ds(0, 2)], out_sem)
    out_copy.start()
    for tap in range(3):
        part = slice(tap * width, (tap + 1) * width)
        term = dot(jnp.concatenate([flipped[2 - tap], flipped[3 - tap]], 1), slope)
        total[part, :] = (wpart[part, :] + term) * scale
    pieces, rows, _ = terms_ref.shape
    for piece in range(pieces):
        terms_ref[piece] = total[piece_at(piece, rows)].astype(jnp.bfloat16)
    out_copy.wait()


def back_kernel(grad, head, halo, w, out_hbm, out, out_sem):
    count, pixels, width = out.shape
    weights = jnp.concatenate([w[tap].T for tap in range(3)], 0)
    size = 3
    for start in range(0, count, size):
        end = min(start + size, count)
        lines = []
        for tap in range(3):
            picked = []
            for t in range(start + tap, end + tap):
                picked.append(head[t] if t < 2 else grad[t] if t < count else halo[t - count])
            lines.append(jnp.concatenate(picked, 0))
        total = dot(jnp.concatenate(lines, 1), weights)
        out[start:end] = total.astype(jnp.bfloat16).reshape(end - start, pixels, width)
        part = pl.ds(start, end - start)
        pltpu.make_async_copy(out.at[part], out_hbm.at[part], out_sem.at[start // size]).start()
    for start in range(0, count, size):
        part = pl.ds(start, min(size, count - start))
        pltpu.make_async_copy(out.at[part], out_hbm.at[part], out_sem.at[start // size]).wait()


def spread_sum_kernel(in_ref, *refs):
    out_ref = refs[-1]
    total = jnp.sum(in_ref[...].astype(jnp.float32), 0).astype(jnp.bfloat16)
    for piece in range(out_ref.shape[0]):
        out_ref[piece] = total


def last_kernel(in_ref, out_ref):
    pieces, rows, _ = in_ref.shape
    for piece in range(pieces):
        out_ref[piece_at(piece, rows)] = in_ref[piece].astype(jnp.float32)


def call(kernel, out_shape, in_specs, out_specs, scratch=(), aliases={}, flops=0, moved=0):
    return pl.pallas_call(
        kernel,
        out_shape=out_shape,
        in_specs=in_specs,
        out_specs=out_specs,
        scratch_shapes=list(scratch),
        input_output_aliases=aliases,
        compiler_params=pltpu.CompilerParams(vmem_limit_bytes=VMEM_LIMIT),
        cost_estimate=pl.CostEstimate(flops=flops, bytes_accessed=moved, transcendentals=0),
    )


def passed_along(value, axis, steps):
    count = lax.axis_size(axis)
    first, last = (max(0, -steps), min(count, count - steps))
    return lax.ppermute(value, axis, [(source, source + steps) for source in range(first, last)])


def exchange(value, axes):
    return lax.all_to_all(value, axes, 0, 0, tiled=True)


def spread_sum(terms, copies, *passed):
    sds = jax.ShapeDtypeStruct
    shapes = [sds(value.shape, value.dtype) for value in passed]
    shapes.append(sds((copies,) + terms.shape[1:], terms.dtype))
    anywhere = [pl.BlockSpec(memory_space=pl.ANY)] * len(passed)
    aliases = {i + 1: i for i in range(len(passed))}
    return call(spread_sum_kernel, shapes, [VMEM] + anywhere, anywhere + [VMEM], aliases=aliases)(
        terms, *passed
    )


def local(lengths, frames, weights, cotangent):
    bf16, f32 = jnp.bfloat16, jnp.float32
    clip, cot = frames[0], cotangent[0]
    count, pixels, chans = clip.shape
    frame = (count, pixels, chans)
    sds = jax.ShapeDtypeStruct
    dma = pltpu.SemaphoreType.DMA
    halo = passed_along(clip[count - 2 :], "x", 1)
    size = pixels * chans * 2
    work = 2 * pixels * chans * chans
    output, grad, wpart = call(
        body_kernel,
        (sds(frame, bf16), sds(frame, bf16), sds((3 * chans, chans), f32)),
        [SMEM, VMEM, VMEM, VMEM],
        (HBM, VMEM, VMEM),
        scratch=[pltpu.VMEM(frame, bf16), pltpu.VMEM((chans, count * pixels), bf16), dma((2,))],
        flops=(count - 2) * 6 * work,
        moved=36 * size,
    )(lengths, clip, cot, weights)
    total_rows = lax.axis_size(MESH_AXES) * count * pixels
    pieces, terms_of = lax.axis_size(SCATTER), lax.axis_size(SUM)
    output, head, terms = call(
        functools.partial(head_kernel, 1.0 / math.sqrt(total_rows), count),
        (
            sds(frame, bf16),
            sds((2, pixels, chans), bf16),
            sds((pieces, 3 * chans * chans // LANES // pieces, LANES), bf16),
        ),
        [SMEM, VMEM, VMEM, VMEM, VMEM, VMEM, HBM],
        (HBM, VMEM, VMEM),
        scratch=[
            pltpu.VMEM((2, pixels, chans), bf16),
            pltpu.VMEM((3 * chans, chans), f32),
            dma,
        ],
        aliases={6: 0},
        flops=12 * work,
        moved=16 * size,
    )(lengths, halo, clip, cot, weights, wpart, output)

    head, terms = spread_sum(exchange(terms, SCATTER), terms_of, head)
    following = passed_along(head, "x", -1)
    following, terms = spread_sum(exchange(terms, SUM), pieces, following)
    terms = exchange(terms, SCATTER)
    input_grad = call(
        back_kernel,
        sds(frame, bf16),
        [VMEM, VMEM, VMEM, VMEM],
        HBM,
        scratch=[pltpu.VMEM(frame, bf16), dma((-(-count // 3),))],
        flops=count * 3 * work,
        moved=22 * size,
    )(grad, head, following, weights)
    weight_grad = call(last_kernel, sds((3 * chans, chans), f32), [VMEM], VMEM)(terms)
    return (output[None], input_grad[None], weight_grad.reshape(3, chans, chans))


def solution(mesh):
    dp, tm = mesh.devices.shape
    side = math.isqrt(dp // 2)
    fine = Mesh(mesh.devices.reshape(side // 2, 2, -1, 2, 2, tm), MESH_AXES)
    data = P(MESH_AXES[:5], "x", None, None)
    in_specs = (P(MESH_AXES[:5]), data, P(), data)
    out_specs = (data, data, P())
    return jax.shard_map(local, mesh=fine, in_specs=in_specs, out_specs=out_specs, check_vma=False)
```

```python
import functools
import math

import jax
import jax.numpy as jnp
from jax import lax
from jax.experimental import pallas as pl
from jax.experimental.pallas import tpu as pltpu
from jax.sharding import Mesh, PartitionSpec as P

LANES = 128
MESH_AXES = ("far_z", "z", "far_y", "y", "c", "x")
SCATTER = ("c", "x", "y", "z")
SUM = ("far_z", "far_y")
VMEM_LIMIT = 40 * 1024 * 1024
VMEM = pl.BlockSpec(memory_space=pltpu.VMEM)
SMEM = pl.BlockSpec(memory_space=pltpu.SMEM)
HBM = pl.BlockSpec(memory_space=pltpu.HBM)
ROWS = (((1,), (0,)), ((), ()))
COLS = (((1,), (1,)), ((), ()))


def dot(a, b, dims=ROWS):
    return lax.dot_general(a, b, dims, preferred_element_type=jnp.float32)


def activate(pre, cot, keep):
    sig = 0.5 * jnp.tanh(0.5 * pre) + 0.5
    value = keep * (pre * sig)
    slope = (keep * cot.astype(jnp.float32)) * (sig * (1.0 + pre * (1.0 - sig)))
    return value.astype(jnp.bfloat16), slope.astype(jnp.bfloat16)


def taps_of(frames, t, size):
    return jnp.concatenate([rows_of(frames[t - tap : t - tap + size]) for tap in range(3)], 1)


def rows_of(frames):
    return frames.reshape(-1, frames.shape[-1])


def body_kernel(length_ref, frames, cot, w, out_hbm, grad, wsum_ref, out, flipped, out_sem):
    count, pixels, width = frames.shape
    middle = 2 + (count - 2) // 2
    groups = [(2, middle), (middle, count)]
    stacked = rows_of(w[...])
    pre = [dot(taps_of(frames, 2, middle - 2), stacked)]
    pre.append(dot(taps_of(frames, middle, count - middle), stacked))
    for t in range(count):
        flipped[:, t * pixels : (t + 1) * pixels] = frames[t].T
    left = frames_left(length_ref, count)
    done = []
    for g, (start, end) in enumerate(groups):
        slopes = []
        for t in range(start, end):
            rows = slice((t - start) * pixels, (t - start + 1) * pixels)
            keep = (t < left).astype(jnp.float32)
            value, slope = activate(pre[g][rows], cot[t], keep)
            out[t] = value
            grad[t] = slope
            slopes.append(slope)
        part = pl.ds(start, end - start)
        done.append(pltpu.make_async_copy(out.at[part], out_hbm.at[part], out_sem.at[g]))
        done[-1].start()
        slope = jnp.concatenate(slopes, 0)
        for tap in range(3):
            term = dot(flipped[:, (start - tap) * pixels : (end - tap) * pixels], slope)
            part = slice(tap * width, (tap + 1) * width)
            wsum_ref[part, :] = term if g == 0 else wsum_ref[part, :] + term
    for copy in done:
        copy.wait()


def frames_left(length_ref, count):
    return length_ref[0] - lax.axis_index("x") * count


def piece_at(piece, rows):
    row, col = divmod(piece, 2)
    return slice(row * rows, (row + 1) * rows), slice(col * LANES, (col + 1) * LANES)


def head_kernel(
    scale, count, length_ref, halo, frames, cot, w, wpart, out_in, out_hbm, head_ref, terms_ref,
    out, total, out_sem,
):
    del out_in
    pixels, width = halo.shape[1:]
    left = frames_left(length_ref, count)
    back = [halo[0], halo[1], frames[0], frames[1]]
    lines = [jnp.concatenate(back[2 - tap : 4 - tap], 0) for tap in range(3)]
    pre = dot(jnp.concatenate(lines, 1), rows_of(w[...]))
    flipped = [frame.T for frame in back]
    slopes = []
    for t in range(2):
        keep = (t < left).astype(jnp.float32)
        value, slope = activate(pre[t * pixels : (t + 1) * pixels], cot[t], keep)
        out[t] = value
        head_ref[t] = slope
        slopes.append(slope)
    slope = jnp.concatenate(slopes, 0)
    out_copy = pltpu.make_async_copy(out, out_hbm.at[pl.ds(0, 2)], out_sem)
    out_copy.start()
    for tap in range(3):
        part = slice(tap * width, (tap + 1) * width)
        term = dot(jnp.concatenate([flipped[2 - tap], flipped[3 - tap]], 1), slope)
        total[part, :] = (wpart[part, :] + term) * scale
    pieces, rows, _ = terms_ref.shape
    for piece in range(pieces):
        terms_ref[piece] = total[piece_at(piece, rows)].astype(jnp.bfloat16)
    out_copy.wait()


def back_kernel(grad, head, halo, w, out_hbm, out, out_sem):
    count, pixels, width = out.shape
    weights = jnp.concatenate([w[tap].T for tap in range(3)], 0)
    size = 3
    for start in range(0, count, size):
        end = min(start + size, count)
        lines = []
        for tap in range(3):
            picked = []
            for t in range(start + tap, end + tap):
                picked.append(head[t] if t < 2 else grad[t] if t < count else halo[t - count])
            lines.append(jnp.concatenate(picked, 0))
        total = dot(jnp.concatenate(lines, 1), weights)
        out[start:end] = total.astype(jnp.bfloat16).reshape(end - start, pixels, width)
        part = pl.ds(start, end - start)
        pltpu.make_async_copy(out.at[part], out_hbm.at[part], out_sem.at[start // size]).start()
    for start in range(0, count, size):
        part = pl.ds(start, min(size, count - start))
        pltpu.make_async_copy(out.at[part], out_hbm.at[part], out_sem.at[start // size]).wait()


def spread_sum_kernel(in_ref, *refs):
    out_ref = refs[-1]
    total = jnp.sum(in_ref[...].astype(jnp.float32), 0).astype(jnp.bfloat16)
    for piece in range(out_ref.shape[0]):
        out_ref[piece] = total


def last_kernel(in_ref, out_ref):
    pieces, rows, _ = in_ref.shape
    for piece in range(pieces):
        out_ref[piece_at(piece, rows)] = in_ref[piece].astype(jnp.float32)


def call(kernel, out_shape, in_specs, out_specs, scratch=(), aliases={}, flops=0, moved=0):
    return pl.pallas_call(
        kernel,
        out_shape=out_shape,
        in_specs=in_specs,
        out_specs=out_specs,
        scratch_shapes=list(scratch),
        input_output_aliases=aliases,
        compiler_params=pltpu.CompilerParams(vmem_limit_bytes=VMEM_LIMIT),
        cost_estimate=pl.CostEstimate(flops=flops, bytes_accessed=moved, transcendentals=0),
    )


def passed_along(value, axis, steps):
    count = lax.axis_size(axis)
    first, last = (max(0, -steps), min(count, count - steps))
    return lax.ppermute(value, axis, [(source, source + steps) for source in range(first, last)])


def exchange(value, axes):
    return lax.all_to_all(value, axes, 0, 0, tiled=True)


def spread_sum(terms, copies, *passed):
    sds = jax.ShapeDtypeStruct
    shapes = [sds(value.shape, value.dtype) for value in passed]
    shapes.append(sds((copies,) + terms.shape[1:], terms.dtype))
    anywhere = [pl.BlockSpec(memory_space=pl.ANY)] * len(passed)
    aliases = {i + 1: i for i in range(len(passed))}
    return call(spread_sum_kernel, shapes, [VMEM] + anywhere, anywhere + [VMEM], aliases=aliases)(
        terms, *passed
    )


def local(lengths, frames, weights, cotangent):
    bf16, f32 = jnp.bfloat16, jnp.float32
    clip, cot = frames[0], cotangent[0]
    count, pixels, chans = clip.shape
    frame = (count, pixels, chans)
    sds = jax.ShapeDtypeStruct
    dma = pltpu.SemaphoreType.DMA
    halo = passed_along(clip[count - 2 :], "x", 1)
    size = pixels * chans * 2
    work = 2 * pixels * chans * chans
    output, grad, wpart = call(
        body_kernel,
        (sds(frame, bf16), sds(frame, bf16), sds((3 * chans, chans), f32)),
        [SMEM, VMEM, VMEM, VMEM],
        (HBM, VMEM, VMEM),
        scratch=[pltpu.VMEM(frame, bf16), pltpu.VMEM((chans, count * pixels), bf16), dma((2,))],
        flops=(count - 2) * 6 * work,
        moved=36 * size,
    )(lengths, clip, cot, weights)
    total_rows = lax.axis_size(MESH_AXES) * count * pixels
    pieces, terms_of = lax.axis_size(SCATTER), lax.axis_size(SUM)
    output, head, terms = call(
        functools.partial(head_kernel, 1.0 / math.sqrt(total_rows), count),
        (
            sds(frame, bf16),
            sds((2, pixels, chans), bf16),
            sds((pieces, 3 * chans * chans // LANES // pieces, LANES), bf16),
        ),
        [SMEM, VMEM, VMEM, VMEM, VMEM, VMEM, HBM],
        (HBM, VMEM, VMEM),
        scratch=[
            pltpu.VMEM((2, pixels, chans), bf16),
            pltpu.VMEM((3 * chans, chans), f32),
            dma,
        ],
        aliases={6: 0},
        flops=12 * work,
        moved=16 * size,
    )(lengths, halo, clip, cot, weights, wpart, output)

    following = passed_along(head, "x", -1)
    following, terms = spread_sum(exchange(terms, SCATTER), terms_of, following)
    (terms,) = spread_sum(exchange(terms, SUM), pieces)
    terms = exchange(terms, SCATTER)
    input_grad = call(
        back_kernel,
        sds(frame, bf16),
        [VMEM, VMEM, VMEM, VMEM],
        HBM,
        scratch=[pltpu.VMEM(frame, bf16), dma((-(-count // 3),))],
        flops=count * 3 * work,
        moved=22 * size,
    )(grad, head, following, weights)
    weight_grad = call(last_kernel, sds((3 * chans, chans), f32), [VMEM], VMEM)(terms)
    return (output[None], input_grad[None], weight_grad.reshape(3, chans, chans))


def solution(mesh):
    dp, tm = mesh.devices.shape
    side = math.isqrt(dp // 2)
    fine = Mesh(mesh.devices.reshape(side // 2, 2, -1, 2, 2, tm), MESH_AXES)
    data = P(MESH_AXES[:5], "x", None, None)
    in_specs = (P(MESH_AXES[:5]), data, P(), data)
    out_specs = (data, data, P())
    return jax.shard_map(local, mesh=fine, in_specs=in_specs, out_specs=out_specs, check_vma=False)
```

```python
import functools
import math

import jax
import jax.numpy as jnp
from jax import lax
from jax.experimental import pallas as pl
from jax.experimental.pallas import tpu as pltpu
from jax.sharding import Mesh, PartitionSpec as P

LANES = 128
MESH_AXES = ("far_z", "z", "far_y", "y", "c", "x")
SCATTER = ("z", "y", "c", "x")
SUM = ("far_z", "far_y")
VMEM_LIMIT = 40 * 1024 * 1024
VMEM = pl.BlockSpec(memory_space=pltpu.VMEM)
SMEM = pl.BlockSpec(memory_space=pltpu.SMEM)
HBM = pl.BlockSpec(memory_space=pltpu.HBM)
ROWS = (((1,), (0,)), ((), ()))
COLS = (((1,), (1,)), ((), ()))


def dot(a, b, dims=ROWS):
    return lax.dot_general(a, b, dims, preferred_element_type=jnp.float32)


def activate(pre, cot, keep):
    sig = 0.5 * jnp.tanh(0.5 * pre) + 0.5
    value = keep * (pre * sig)
    slope = (keep * cot.astype(jnp.float32)) * (sig * (1.0 + pre * (1.0 - sig)))
    return value.astype(jnp.bfloat16), slope.astype(jnp.bfloat16)


def taps_of(frames, t, size):
    return jnp.concatenate([rows_of(frames[t - tap : t - tap + size]) for tap in range(3)], 1)


def rows_of(frames):
    return frames.reshape(-1, frames.shape[-1])


def body_kernel(length_ref, frames, cot, w, out_hbm, grad, wsum_ref, out, flipped, out_sem):
    count, pixels, width = frames.shape
    middle = 2 + (count - 2) // 2
    groups = [(2, middle), (middle, count)]
    stacked = rows_of(w[...])
    pre = [dot(taps_of(frames, 2, middle - 2), stacked)]
    pre.append(dot(taps_of(frames, middle, count - middle), stacked))
    for t in range(count):
        flipped[:, t * pixels : (t + 1) * pixels] = frames[t].T
    left = frames_left(length_ref, count)
    done = []
    for g, (start, end) in enumerate(groups):
        slopes = []
        for t in range(start, end):
            rows = slice((t - start) * pixels, (t - start + 1) * pixels)
            keep = (t < left).astype(jnp.float32)
            value, slope = activate(pre[g][rows], cot[t], keep)
            out[t] = value
            grad[t] = slope
            slopes.append(slope)
        part = pl.ds(start, end - start)
        done.append(pltpu.make_async_copy(out.at[part], out_hbm.at[part], out_sem.at[g]))
        done[-1].start()
        slope = jnp.concatenate(slopes, 0)
        for tap in range(3):
            term = dot(flipped[:, (start - tap) * pixels : (end - tap) * pixels], slope)
            part = slice(tap * width, (tap + 1) * width)
            wsum_ref[part, :] = term if g == 0 else wsum_ref[part, :] + term
    for copy in done:
        copy.wait()


def frames_left(length_ref, count):
    return length_ref[0] - lax.axis_index("x") * count


def piece_at(piece, rows):
    row, col = divmod(piece, 2)
    return slice(row * rows, (row + 1) * rows), slice(col * LANES, (col + 1) * LANES)


def head_kernel(
    scale, count, length_ref, halo, frames, cot, w, wpart, out_in, out_hbm, head_ref, terms_ref,
    out, total, out_sem,
):
    del out_in
    pixels, width = halo.shape[1:]
    left = frames_left(length_ref, count)
    back = [halo[0], halo[1], frames[0], frames[1]]
    lines = [jnp.concatenate(back[2 - tap : 4 - tap], 0) for tap in range(3)]
    pre = dot(jnp.concatenate(lines, 1), rows_of(w[...]))
    flipped = [frame.T for frame in back]
    slopes = []
    for t in range(2):
        keep = (t < left).astype(jnp.float32)
        value, slope = activate(pre[t * pixels : (t + 1) * pixels], cot[t], keep)
        out[t] = value
        head_ref[t] = slope
        slopes.append(slope)
    slope = jnp.concatenate(slopes, 0)
    out_copy = pltpu.make_async_copy(out, out_hbm.at[pl.ds(0, 2)], out_sem)
    out_copy.start()
    for tap in range(3):
        part = slice(tap * width, (tap + 1) * width)
        term = dot(jnp.concatenate([flipped[2 - tap], flipped[3 - tap]], 1), slope)
        total[part, :] = (wpart[part, :] + term) * scale
    pieces, rows, _ = terms_ref.shape
    for piece in range(pieces):
        terms_ref[piece] = total[piece_at(piece, rows)].astype(jnp.bfloat16)
    out_copy.wait()


def back_kernel(grad, head, halo, w, out_hbm, out, out_sem):
    count, pixels, width = out.shape
    weights = jnp.concatenate([w[tap].T for tap in range(3)], 0)
    size = 3
    for start in range(0, count, size):
        end = min(start + size, count)
        lines = []
        for tap in range(3):
            picked = []
            for t in range(start + tap, end + tap):
                picked.append(head[t] if t < 2 else grad[t] if t < count else halo[t - count])
            lines.append(jnp.concatenate(picked, 0))
        total = dot(jnp.concatenate(lines, 1), weights)
        out[start:end] = total.astype(jnp.bfloat16).reshape(end - start, pixels, width)
        part = pl.ds(start, end - start)
        pltpu.make_async_copy(out.at[part], out_hbm.at[part], out_sem.at[start // size]).start()
    for start in range(0, count, size):
        part = pl.ds(start, min(size, count - start))
        pltpu.make_async_copy(out.at[part], out_hbm.at[part], out_sem.at[start // size]).wait()


def spread_sum_kernel(in_ref, *refs):
    out_ref = refs[-1]
    total = jnp.sum(in_ref[...].astype(jnp.float32), 0).astype(jnp.bfloat16)
    for piece in range(out_ref.shape[0]):
        out_ref[piece] = total


def last_kernel(in_ref, out_ref):
    pieces, rows, _ = in_ref.shape
    for piece in range(pieces):
        out_ref[piece_at(piece, rows)] = in_ref[piece].astype(jnp.float32)


def call(kernel, out_shape, in_specs, out_specs, scratch=(), aliases={}, flops=0, moved=0):
    return pl.pallas_call(
        kernel,
        out_shape=out_shape,
        in_specs=in_specs,
        out_specs=out_specs,
        scratch_shapes=list(scratch),
        input_output_aliases=aliases,
        compiler_params=pltpu.CompilerParams(vmem_limit_bytes=VMEM_LIMIT),
        cost_estimate=pl.CostEstimate(flops=flops, bytes_accessed=moved, transcendentals=0),
    )


def passed_along(value, axis, steps):
    count = lax.axis_size(axis)
    first, last = (max(0, -steps), min(count, count - steps))
    return lax.ppermute(value, axis, [(source, source + steps) for source in range(first, last)])


def exchange(value, axes):
    return lax.all_to_all(value, axes, 0, 0, tiled=True)


def spread_sum(terms, copies, *passed):
    sds = jax.ShapeDtypeStruct
    shapes = [sds(value.shape, value.dtype) for value in passed]
    shapes.append(sds((copies,) + terms.shape[1:], terms.dtype))
    anywhere = [pl.BlockSpec(memory_space=pl.ANY)] * len(passed)
    aliases = {i + 1: i for i in range(len(passed))}
    return call(spread_sum_kernel, shapes, [VMEM] + anywhere, anywhere + [VMEM], aliases=aliases)(
        terms, *passed
    )


def local(lengths, frames, weights, cotangent):
    bf16, f32 = jnp.bfloat16, jnp.float32
    clip, cot = frames[0], cotangent[0]
    count, pixels, chans = clip.shape
    frame = (count, pixels, chans)
    sds = jax.ShapeDtypeStruct
    dma = pltpu.SemaphoreType.DMA
    halo = passed_along(clip[count - 2 :], "x", 1)
    size = pixels * chans * 2
    work = 2 * pixels * chans * chans
    output, grad, wpart = call(
        body_kernel,
        (sds(frame, bf16), sds(frame, bf16), sds((3 * chans, chans), f32)),
        [SMEM, VMEM, VMEM, VMEM],
        (HBM, VMEM, VMEM),
        scratch=[pltpu.VMEM(frame, bf16), pltpu.VMEM((chans, count * pixels), bf16), dma((2,))],
        flops=(count - 2) * 6 * work,
        moved=36 * size,
    )(lengths, clip, cot, weights)
    total_rows = lax.axis_size(MESH_AXES) * count * pixels
    pieces, terms_of = lax.axis_size(SCATTER), lax.axis_size(SUM)
    output, head, terms = call(
        functools.partial(head_kernel, 1.0 / math.sqrt(total_rows), count),
        (
            sds(frame, bf16),
            sds((2, pixels, chans), bf16),
            sds((pieces, 3 * chans * chans // LANES // pieces, LANES), bf16),
        ),
        [SMEM, VMEM, VMEM, VMEM, VMEM, VMEM, HBM],
        (HBM, VMEM, VMEM),
        scratch=[
            pltpu.VMEM((2, pixels, chans), bf16),
            pltpu.VMEM((3 * chans, chans), f32),
            dma,
        ],
        aliases={6: 0},
        flops=12 * work,
        moved=16 * size,
    )(lengths, halo, clip, cot, weights, wpart, output)

    head, terms = spread_sum(exchange(terms, SCATTER), terms_of, head)
    following = passed_along(head, "x", -1)
    following, terms = spread_sum(exchange(terms, SUM), pieces, following)
    terms = exchange(terms, SCATTER)
    input_grad = call(
        back_kernel,
        sds(frame, bf16),
        [VMEM, VMEM, VMEM, VMEM],
        HBM,
        scratch=[pltpu.VMEM(frame, bf16), dma((-(-count // 3),))],
        flops=count * 3 * work,
        moved=22 * size,
    )(grad, head, following, weights)
    weight_grad = call(last_kernel, sds((3 * chans, chans), f32), [VMEM], VMEM)(terms)
    return (output[None], input_grad[None], weight_grad.reshape(3, chans, chans))


def solution(mesh):
    dp, tm = mesh.devices.shape
    side = math.isqrt(dp // 2)
    fine = Mesh(mesh.devices.reshape(side // 2, 2, -1, 2, 2, tm), MESH_AXES)
    data = P(MESH_AXES[:5], "x", None, None)
    in_specs = (P(MESH_AXES[:5]), data, P(), data)
    out_specs = (data, data, P())
    return jax.shard_map(local, mesh=fine, in_specs=in_specs, out_specs=out_specs, check_vma=False)
```

```python
import functools
import math

import jax
import jax.numpy as jnp
from jax import lax
from jax.experimental import pallas as pl
from jax.experimental.pallas import tpu as pltpu
from jax.sharding import Mesh, PartitionSpec as P

LANES = 128
MESH_AXES = ("far_z", "z", "far_y", "y", "c", "x")
SCATTER = ("z", "y", "c", "x")
SUM = ("far_z", "far_y")
VMEM_LIMIT = 40 * 1024 * 1024
VMEM = pl.BlockSpec(memory_space=pltpu.VMEM)
SMEM = pl.BlockSpec(memory_space=pltpu.SMEM)
HBM = pl.BlockSpec(memory_space=pltpu.HBM)
ROWS = (((1,), (0,)), ((), ()))
COLS = (((1,), (1,)), ((), ()))


def dot(a, b, dims=ROWS):
    return lax.dot_general(a, b, dims, preferred_element_type=jnp.float32)


def activate(pre, cot, keep):
    sig = 0.5 * jnp.tanh(0.5 * pre) + 0.5
    value = keep * (pre * sig)
    slope = (keep * cot.astype(jnp.float32)) * (sig * (1.0 + pre * (1.0 - sig)))
    return value.astype(jnp.bfloat16), slope.astype(jnp.bfloat16)


def taps_of(frames, t, size):
    return jnp.concatenate([rows_of(frames[t - tap : t - tap + size]) for tap in range(3)], 1)


def rows_of(frames):
    return frames.reshape(-1, frames.shape[-1])


def body_kernel(length_ref, frames, cot, w, out_hbm, grad, wsum_ref, out, flipped, out_sem):
    count, pixels, width = frames.shape
    middle = 2 + (count - 2) // 2
    groups = [(2, middle), (middle, count)]
    stacked = rows_of(w[...])
    pre = [dot(taps_of(frames, 2, middle - 2), stacked)]
    pre.append(dot(taps_of(frames, middle, count - middle), stacked))
    for t in range(count):
        flipped[:, t * pixels : (t + 1) * pixels] = frames[t].T
    left = frames_left(length_ref, count)
    done = []
    for g, (start, end) in enumerate(groups):
        slopes = []
        for t in range(start, end):
            rows = slice((t - start) * pixels, (t - start + 1) * pixels)
            keep = (t < left).astype(jnp.float32)
            value, slope = activate(pre[g][rows], cot[t], keep)
            out[t] = value
            grad[t] = slope
            slopes.append(slope)
        part = pl.ds(start, end - start)
        done.append(pltpu.make_async_copy(out.at[part], out_hbm.at[part], out_sem.at[g]))
        done[-1].start()
        slope = jnp.concatenate(slopes, 0)
        for tap in range(3):
            term = dot(flipped[:, (start - tap) * pixels : (end - tap) * pixels], slope)
            part = slice(tap * width, (tap + 1) * width)
            wsum_ref[part, :] = term if g == 0 else wsum_ref[part, :] + term
    for copy in done:
        copy.wait()


def frames_left(length_ref, count):
    return length_ref[0] - lax.axis_index("x") * count


def piece_at(piece, rows):
    row, col = divmod(piece, 2)
    return slice(row * rows, (row + 1) * rows), slice(col * LANES, (col + 1) * LANES)


def head_kernel(
    scale, count, length_ref, halo, frames, cot, w, wpart, out_in, out_hbm, head_ref, terms_ref,
    out, out_sem,
):
    del out_in
    pixels, width = halo.shape[1:]
    left = frames_left(length_ref, count)
    back = [halo[0], halo[1], frames[0], frames[1]]
    lines = [jnp.concatenate(back[2 - tap : 4 - tap], 0) for tap in range(3)]
    pre = dot(jnp.concatenate(lines, 1), rows_of(w[...]))
    flipped = [frame.T for frame in back]
    slopes = []
    for t in range(2):
        keep = (t < left).astype(jnp.float32)
        value, slope = activate(pre[t * pixels : (t + 1) * pixels], cot[t], keep)
        out[t] = value
        head_ref[t] = slope
        slopes.append(slope)
    slope = jnp.concatenate(slopes, 0)
    out_copy = pltpu.make_async_copy(out, out_hbm.at[pl.ds(0, 2)], out_sem)
    out_copy.start()
    pieces = terms_ref.shape[0]
    rows = terms_ref.shape[1] // 3
    for tap in range(3):
        part = slice(tap * width, (tap + 1) * width)
        term = dot(jnp.concatenate([flipped[2 - tap], flipped[3 - tap]], 1), slope)
        total = ((wpart[part, :] + term) * scale).astype(jnp.bfloat16)
        for piece in range(pieces):
            terms_ref[piece, tap * rows : (tap + 1) * rows, :] = total[piece_at(piece, rows)]
    out_copy.wait()


def back_kernel(grad, head, halo, w, out_hbm, out, out_sem):
    count, pixels, width = out.shape
    weights = jnp.concatenate([w[tap].T for tap in range(3)], 0)
    size = 3
    for start in range(0, count, size):
        end = min(start + size, count)
        lines = []
        for tap in range(3):
            picked = []
            for t in range(start + tap, end + tap):
                picked.append(head[t] if t < 2 else grad[t] if t < count else halo[t - count])
            lines.append(jnp.concatenate(picked, 0))
        total = dot(jnp.concatenate(lines, 1), weights)
        out[start:end] = total.astype(jnp.bfloat16).reshape(end - start, pixels, width)
        part = pl.ds(start, end - start)
        pltpu.make_async_copy(out.at[part], out_hbm.at[part], out_sem.at[start // size]).start()
    for start in range(0, count, size):
        part = pl.ds(start, min(size, count - start))
        pltpu.make_async_copy(out.at[part], out_hbm.at[part], out_sem.at[start // size]).wait()


def spread_sum_kernel(in_ref, *refs):
    out_ref = refs[-1]
    total = jnp.sum(in_ref[...].astype(jnp.float32), 0).astype(jnp.bfloat16)
    for piece in range(out_ref.shape[0]):
        out_ref[piece] = total


def last_kernel(in_ref, out_hbm, out, out_sem):
    pieces, rows = in_ref.shape[0], in_ref.shape[1] // 3
    copies = []
    for tap in range(3):
        for piece in range(pieces):
            across, along = piece_at(piece, rows)
            out[tap, across, along] = in_ref[piece, tap * rows : (tap + 1) * rows, :].astype(jnp.float32)
        copies.append(pltpu.make_async_copy(out.at[tap], out_hbm.at[tap], out_sem.at[tap]))
        copies[-1].start()
    for copy in copies:
        copy.wait()


def call(kernel, out_shape, in_specs, out_specs, scratch=(), aliases={}, flops=0, moved=0):
    return pl.pallas_call(
        kernel,
        out_shape=out_shape,
        in_specs=in_specs,
        out_specs=out_specs,
        scratch_shapes=list(scratch),
        input_output_aliases=aliases,
        compiler_params=pltpu.CompilerParams(vmem_limit_bytes=VMEM_LIMIT),
        cost_estimate=pl.CostEstimate(flops=flops, bytes_accessed=moved, transcendentals=0),
    )


def passed_along(value, axis, steps):
    count = lax.axis_size(axis)
    first, last = (max(0, -steps), min(count, count - steps))
    return lax.ppermute(value, axis, [(source, source + steps) for source in range(first, last)])


def exchange(value, axes):
    return lax.all_to_all(value, axes, 0, 0, tiled=True)


def spread_sum(terms, copies, *passed):
    sds = jax.ShapeDtypeStruct
    shapes = [sds(value.shape, value.dtype) for value in passed]
    shapes.append(sds((copies,) + terms.shape[1:], terms.dtype))
    anywhere = [pl.BlockSpec(memory_space=pl.ANY)] * len(passed)
    aliases = {i + 1: i for i in range(len(passed))}
    return call(spread_sum_kernel, shapes, [VMEM] + anywhere, anywhere + [VMEM], aliases=aliases)(
        terms, *passed
    )


def local(lengths, frames, weights, cotangent):
    bf16, f32 = jnp.bfloat16, jnp.float32
    clip, cot = frames[0], cotangent[0]
    count, pixels, chans = clip.shape
    frame = (count, pixels, chans)
    sds = jax.ShapeDtypeStruct
    dma = pltpu.SemaphoreType.DMA
    halo = passed_along(clip[count - 2 :], "x", 1)
    size = pixels * chans * 2
    work = 2 * pixels * chans * chans
    output, grad, wpart = call(
        body_kernel,
        (sds(frame, bf16), sds(frame, bf16), sds((3 * chans, chans), f32)),
        [SMEM, VMEM, VMEM, VMEM],
        (HBM, VMEM, VMEM),
        scratch=[pltpu.VMEM(frame, bf16), pltpu.VMEM((chans, count * pixels), bf16), dma((2,))],
        flops=(count - 2) * 6 * work,
        moved=36 * size,
    )(lengths, clip, cot, weights)
    total_rows = lax.axis_size(MESH_AXES) * count * pixels
    pieces, terms_of = lax.axis_size(SCATTER), lax.axis_size(SUM)
    output, head, terms = call(
        functools.partial(head_kernel, 1.0 / math.sqrt(total_rows), count),
        (
            sds(frame, bf16),
            sds((2, pixels, chans), bf16),
            sds((pieces, 3 * chans * chans // LANES // pieces, LANES), bf16),
        ),
        [SMEM, VMEM, VMEM, VMEM, VMEM, VMEM, HBM],
        (HBM, VMEM, VMEM),
        scratch=[
            pltpu.VMEM((2, pixels, chans), bf16),
            dma,
        ],
        aliases={6: 0},
        flops=12 * work,
        moved=16 * size,
    )(lengths, halo, clip, cot, weights, wpart, output)

    head, terms = spread_sum(exchange(terms, SCATTER), terms_of, head)
    following = passed_along(head, "x", -1)
    following, terms = spread_sum(exchange(terms, SUM), pieces, following)
    terms = exchange(terms, SCATTER)
    input_grad = call(
        back_kernel,
        sds(frame, bf16),
        [VMEM, VMEM, VMEM, VMEM],
        HBM,
        scratch=[pltpu.VMEM(frame, bf16), dma((-(-count // 3),))],
        flops=count * 3 * work,
        moved=22 * size,
    )(grad, head, following, weights)
    shape = (3, chans, chans)
    weight_grad = call(
        last_kernel, sds(shape, f32), [VMEM], HBM, scratch=[pltpu.VMEM(shape, f32), dma((3,))]
    )(terms)
    return (output[None], input_grad[None], weight_grad)


def solution(mesh):
    dp, tm = mesh.devices.shape
    side = math.isqrt(dp // 2)
    fine = Mesh(mesh.devices.reshape(side // 2, 2, -1, 2, 2, tm), MESH_AXES)
    data = P(MESH_AXES[:5], "x", None, None)
    in_specs = (P(MESH_AXES[:5]), data, P(), data)
    out_specs = (data, data, P())
    return jax.shard_map(local, mesh=fine, in_specs=in_specs, out_specs=out_specs, check_vma=False)
```
